256 devices in a mesh: rep: 4 (over y), exp: 64 (over z, x, core).
Axes of the slice: x: 4, y: 4, z: 8, core: 2. Of those that a mesh axis runs over, the one named last changes fastest.
Arguments:
- tokens: bfloat16 [32768, 1024], P(('rep', 'exp')), may hold values from -6 to 6
- gain: float32 [1024], replicated, may hold values from 0.1 to 1.9
- expert_ids: int32 [32768, 2], P(('rep', 'exp')), may hold values from 0 to 63, all different within a row
- gates: float32 [32768, 2], P(('rep', 'exp')), may hold values from 0.1 to 0.9
- w_in: bfloat16 [64, 1024, 4096], P('exp', None, 'rep'), may hold values from -0.1875 to 0.1875
- w_out: bfloat16 [64, 4096, 1024], P('exp', 'rep'), may hold values from -0.09375 to 0.09375
- cotangent: bfloat16 [32768, 1024], P(('rep', 'exp')), may hold values from -6 to 6
Outputs:
- mixed: bfloat16 [32768, 1024], P(('rep', 'exp'))
- grad_tokens: bfloat16 [32768, 1024], P(('rep', 'exp'))
- grad_in: bfloat16 [64, 1024, 4096], P('exp', None, 'rep')
- grad_out: bfloat16 [64, 4096, 1024], P('exp', 'rep')
The draws below stay inside these ranges and needn't reach their ends.
Inputs may be any that keep to these rules, and one draw needn't show every extreme that they name: `expert_ids`: each token names two different experts, and every expert is named by some token.
All inputs are finite; a program needn't handle non-finite values.
Results may differ from the reference program's by a relative error of at most 0.007.
Values may be sent and summed in bfloat16 or wider, within the bound.
A program may use at most 64 MiB of HBM per device.

```python
import jax
import jax.numpy as jnp
from jax import lax

D = 1024
FF = 4096
TOK_DEV = 128
EXPERTS = 64
CAP = 4
TOKENS = 32768
N_REP = 4


def levels(key, shape, cuts, low, top_value):
    def one(axis_at, parts):
        draws = jax.random.uniform(jax.random.fold_in(jax.random.fold_in(key, 6), axis_at), (parts,), jnp.float32, low / len(cuts), top_value / len(cuts))
        return jnp.repeat(jnp.exp(draws), shape[axis_at] // parts).reshape((-1,) + (1,) * (len(shape) - axis_at - 1))

    loudness = one(*cuts[0])
    for cut in cuts[1:]:
        loudness = loudness * one(*cut)
    return loudness


def distinct(stream_key, rows, amount, top, lift):
    order = jax.random.permutation(jax.random.fold_in(stream_key, 1), amount)
    boost = order
    for power in range(3):
        boost = boost * boost // amount
    boost = boost * lift // amount
    tickets = jax.random.randint(jax.random.fold_in(stream_key, 2), (rows, amount), 0, 4096) + boost
    holders = jax.random.permutation(jax.random.fold_in(stream_key, 3), rows)[jnp.arange(amount) % rows]
    tickets = jnp.where(jnp.arange(rows)[:, None] == holders[None, :], 1 << 14, tickets)
    priority = tickets * amount + jnp.arange(amount)
    return lax.top_k(priority.astype(jnp.int32), top)[1].astype(jnp.int32)


def centred(own_key, shape, deviation, most, shards=(), kind=jnp.bfloat16):
    loudness = levels(own_key, shape, shards, -0.22, 0.18) if shards else 1.0
    array = jax.random.normal(own_key, shape, jnp.float32) * deviation * loudness
    return jnp.minimum(jnp.maximum(array, -most), most).astype(kind)


def setup_inputs(seed: int = 0) -> dict:
    streams_of = jax.random.split(jax.random.key(seed), 8)
    return {
        "tokens": centred(streams_of[0], (TOKENS, D), 1.0, 6.0, ((0, 256),)),
        "gain": jnp.clip(1.0 + 0.18 * jax.random.normal(streams_of[1], (D,), jnp.float32), 0.1, 1.9),
        "expert_ids": distinct(streams_of[2], TOKENS, EXPERTS, 2, 256),
        "gates": jnp.clip(0.1 + 0.79999997 * jax.random.uniform(streams_of[3], (TOKENS, 2), jnp.float32) ** levels(streams_of[3], (TOKENS, 2), ((0, 256),), -0.2, 0.2), 0.1, 0.9),
        "w_in": centred(streams_of[4], (EXPERTS, D, FF), D ** -0.5, 0.1875, ((0, 64), (2, 4))),
        "w_out": centred(streams_of[5], (EXPERTS, FF, D), FF ** -0.5, 0.09375, ((0, 64), (1, 4))),
        "cotangent": centred(streams_of[6], (TOKENS, D), 1.0, 6.0, ((0, 256),)),
    }


epsilon = 1e-05

def normalize(entries, gain):
    center = entries - lax.optimization_barrier(jnp.mean(entries, axis=-1, keepdims=True))
    spread = lax.optimization_barrier(jnp.mean(center * center, axis=-1, keepdims=True))
    return center * lax.rsqrt(spread + epsilon) * gain

def activate(entries):
    return jax.nn.gelu(entries, approximate=True)

def grouped_second(hidden, w_second):
    width = FF // N_REP
    total = jnp.zeros((hidden.shape[0], w_second.shape[1]), jnp.float32)
    for group in range(N_REP):
        piece = jnp.dot(hidden[:, group * width:(group + 1) * width], w_second[group * width:(group + 1) * width], preferred_element_type=jnp.float32)
        total = total + piece.astype(jnp.bfloat16).astype(jnp.float32)
    return total.astype(jnp.bfloat16)

def grouped_first(d_pre, w_first):
    width = FF // N_REP
    total = jnp.zeros((d_pre.shape[0], w_first.shape[0]), jnp.float32)
    for group in range(N_REP):
        piece = jnp.dot(d_pre[:, group * width:(group + 1) * width], w_first[:, group * width:(group + 1) * width].T, preferred_element_type=jnp.float32)
        total = total + piece.astype(jnp.bfloat16).astype(jnp.float32)
    return total.astype(jnp.bfloat16)

def per_expert(operands):
    in_rows, grad_rows, w_first, w_second = operands
    preact = jnp.dot(in_rows, w_first, preferred_element_type=jnp.float32)
    activated, act_back = jax.vjp(activate, preact)
    hidden = activated.astype(jnp.bfloat16)
    out_rows = grouped_second(hidden, w_second)
    d_hidden = jnp.dot(grad_rows, w_second.T, preferred_element_type=jnp.float32)
    d_pre = act_back(d_hidden)[0].astype(jnp.bfloat16)
    grad_second = jnp.dot(hidden.T, grad_rows, preferred_element_type=jnp.float32).astype(jnp.bfloat16)
    grad_first = jnp.dot(in_rows.T, d_pre, preferred_element_type=jnp.float32).astype(jnp.bfloat16)
    d_rows = grouped_first(d_pre, w_first)
    return (out_rows, d_rows, grad_first, grad_second)

def reference(tokens, gain, expert_ids, gates, w_in, w_out, cotangent):
    blocks = TOKENS // TOK_DEV
    slots_all = blocks * CAP
    values = tokens.astype(jnp.float32)
    normed, norm_back = jax.vjp(lambda entries: normalize(entries, gain), values)
    normed = normed.astype(jnp.bfloat16)
    chosen = expert_ids.reshape(blocks, 2 * TOK_DEV)
    labels = jnp.arange(EXPERTS, dtype=jnp.int32)
    onehot = (chosen[:, :, None] == labels[None, None, :]).astype(jnp.int32)
    before = jnp.cumsum(onehot, axis=1) - onehot
    ranking = lax.optimization_barrier(jnp.sum(before * onehot, axis=2))
    kept_mask = ranking < CAP
    anchor = jnp.arange(blocks, dtype=jnp.int32)[:, None] * CAP
    slot_row = jnp.where(kept_mask, anchor + ranking, slots_all).reshape(-1).astype(jnp.int32)
    owners = chosen.reshape(-1).astype(jnp.int32)
    paired = jnp.repeat(normed, 2, axis=0)
    scaled = (cotangent.astype(jnp.float32)[:, None, :] * gates[:, :, None]).astype(jnp.bfloat16)
    scaled = scaled.reshape(2 * TOKENS, D)
    blank_rows = jnp.zeros((EXPERTS, slots_all + 1, D), jnp.bfloat16)
    expert_in = blank_rows.at[owners, slot_row].set(paired)[:, :slots_all]
    d_out = blank_rows.at[owners, slot_row].set(scaled)[:, :slots_all]
    out_rows, d_rows, grad_in, grad_out = lax.map(per_expert, (expert_in, d_out, w_in, w_out))
    zero_row = jnp.zeros((EXPERTS, 1, D), jnp.bfloat16)
    out_padded = jnp.concatenate([out_rows, zero_row], axis=1)
    returned = out_padded[owners, slot_row].astype(jnp.float32).reshape(TOKENS, 2, D)
    mixed = (values + lax.optimization_barrier(jnp.sum(gates[:, :, None] * returned, axis=1))).astype(jnp.bfloat16)
    d_padded = jnp.concatenate([d_rows, zero_row], axis=1)
    d_normed = lax.optimization_barrier(jnp.sum(d_padded[owners, slot_row].astype(jnp.float32).reshape(TOKENS, 2, D), axis=1))
    grad_tokens = (cotangent.astype(jnp.float32) + norm_back(d_normed)[0]).astype(jnp.bfloat16)
    return (mixed, grad_tokens, grad_in, grad_out)
```

```python
import functools
import math

import jax
import jax.numpy as jnp
from jax import lax
from jax.experimental import pallas as pl
from jax.experimental.pallas import tpu as pltpu
from jax.sharding import PartitionSpec as P

MESH = pl.DeviceIdType.MESH
F32 = jnp.float32
BF16 = jnp.bfloat16
EPSILON = 1e-05
CAP = 4
UNIT = 2 * CAP
REPS = 4
PLANE = 8
ORDERS = {8: (0, 2, 6, 3, 5, 4, 1, 7), 4: (0, 2, 3, 1), 2: (0, 1)}
ROOT = math.sqrt(2.0 / math.pi)
CUBIC = 0.044715


def dot(left, right, contract=((1,), (0,))):
    return lax.dot_general(left, right, (contract, ((), ())), preferred_element_type=F32)


def kernel(
    order, plane, tile,
    tokens_ref, gain_ref, ids_ref, gates_ref, cot_ref, w_in_ref, w_out_ref,
    mixed_ref, grad_tokens_ref, grad_in_ref, grad_out_ref,
    w_first, w_second, sent, landed, gathered, x_rows, d_rows, hidden, d_pre,
    partial, relay, arrived, back, returned, disp, take, rows_in, xhat, scale, total, g_first, g_second,
    load_sem, disp_send, disp_recv, ag_send, ag_recv, fw_send, fw_recv,
    r1_send, r1_recv, r2_send, r2_recv, ret_send, ret_recv, store_sem,
):
    steps = len(order)
    toks, width = tokens_ref.shape
    group = plane * CAP
    both = 2 * group
    chunk = 2 * REPS * group
    chunks = steps // 2
    places = steps * plane * UNIT
    me_y = lax.axis_index("rep")
    me_e = lax.axis_index("exp")
    me_z = lax.div(me_e, plane)
    me_p = lax.rem(me_e, plane)
    experts = steps * plane
    up = {"rep": lax.rem(me_y + 1, REPS)}
    down = {"rep": lax.rem(me_y + REPS - 1, REPS)}
    sides = (up, down)

    load_first = pltpu.make_async_copy(w_in_ref, w_first, load_sem.at[0])
    load_second = pltpu.make_async_copy(w_out_ref, w_second, load_sem.at[1])
    load_first.start()
    load_second.start()

    barrier = pltpu.get_barrier_semaphore()

    @pl.loop(1, experts)
    def _(s):
        pl.semaphore_signal(barrier, inc=1, device_id={"exp": lax.rem(me_e + s, experts)}, device_id_type=MESH)

    for side in sides:
        pl.semaphore_signal(barrier, inc=1, device_id=side, device_id_type=MESH)

    values = tokens_ref[...].astype(F32)
    center = values - jnp.mean(values, axis=-1, keepdims=True)
    inv = lax.rsqrt(jnp.mean(center * center, axis=-1, keepdims=True) + EPSILON)
    unit = center * inv
    xhat[...] = unit
    scale[...] = inv
    rows_in[0:toks, :] = (unit * gain_ref[...]).astype(BF16)
    cot = cot_ref[...].astype(F32)
    for k in range(2):
        rows_in[(k + 1) * toks:(k + 2) * toks, :] = (cot * gates_ref[:, k:k + 1]).astype(BF16)

    def place_of(k):
        ids = ids_ref[:, k:k + 1]
        z = lax.rem(lax.div(ids, plane) - me_z + steps, steps)
        position = jnp.zeros_like(z)
        for i, away in enumerate(order):
            position = jnp.where(z == away, i, position)
        return position * plane + lax.rem(ids, plane)

    rel = [place_of(k) for k in range(2)]
    labels = lax.broadcasted_iota(jnp.int32, (toks, experts), 1)
    one = [(labels == r).astype(F32) for r in rel]
    earlier = (
        lax.broadcasted_iota(jnp.int32, (toks, toks), 1) < lax.broadcasted_iota(jnp.int32, (toks, toks), 0)
    ).astype(F32).astype(BF16)
    before = dot(earlier, (one[0] + one[1]).astype(BF16))
    q = lax.broadcasted_iota(jnp.int32, (toks, places), 1)
    pick_x, pick_d = [], []
    for k in range(2):
        rank = jnp.sum(before * one[k], axis=1, keepdims=True).astype(jnp.int32)
        target = jnp.where(rank < CAP, rel[k] * UNIT + rank, -UNIT)
        pick_x.append((q == target).astype(F32))
        pick_d.append((q == target + CAP).astype(F32))
    take[0:toks, :] = pick_x[0].astype(BF16)
    take[toks:2 * toks, :] = pick_x[1].astype(BF16)
    take[2 * toks:3 * toks, :] = (pick_d[0] + pick_d[1]).astype(BF16)
    disp[:, 0:toks] = (pick_x[0] + pick_x[1]).T.astype(BF16)
    disp[:, toks:2 * toks] = pick_d[0].T.astype(BF16)
    disp[:, 2 * toks:3 * toks] = pick_d[1].T.astype(BF16)

    def peer(away, p):
        return {"exp": lax.rem(me_z + away + steps, steps) * plane + p}

    rows_at = plane * UNIT

    def dispatch(i):
        piece = dot(disp[i * rows_at:(i + 1) * rows_at, :], rows_in[...])
        sent[i] = piece.reshape(plane, UNIT, width).astype(BF16)
        if i == 0:
            pl.semaphore_wait(barrier, experts - 1 + 2)
        away = order[i]
        if away == 0:
            pltpu.make_async_copy(sent.at[i, me_p], landed.at[i, me_p], disp_recv.at[i]).start()

        @pl.loop(1 if away == 0 else 0, plane)
        def _(s):
            p = lax.rem(me_p + s, plane)
            pltpu.make_async_remote_copy(
                sent.at[i, p], landed.at[i, me_p], disp_send.at[i], disp_recv.at[i],
                device_id=peer(away, p), device_id_type=MESH,
            ).start()

    r = lax.broadcasted_iota(jnp.int32, (both, both), 0)
    c = lax.broadcasted_iota(jnp.int32, (both, both), 1)

    def mixed_row(pure):
        kind = lax.div(pure, group)
        row = lax.rem(pure, group)
        return lax.div(row, CAP) * UNIT + kind * CAP + lax.rem(row, CAP)

    def split_perm():
        return (c == mixed_row(r)).astype(F32).astype(BF16)

    def merge_perm():
        return (r == mixed_row(c)).astype(F32).astype(BF16)

    def whole(ref, sem):
        pltpu.make_async_copy(ref, ref, sem).wait()

    def remote(src, dst, send, recv, where):
        return pltpu.make_async_remote_copy(src, dst, send, recv, device_id=where, device_id_type=MESH)

    def arrive(i):
        whole(landed.at[i], disp_recv.at[i])
        units = landed[i].astype(F32).reshape(both, width).astype(BF16)
        gathered[0, i] = dot(split_perm(), units).astype(BF16)
        for s, slot in ((0, 1), (1, 3)):
            remote(gathered.at[0, i], gathered.at[slot, i], ag_send.at[s], ag_recv.at[s, i], sides[s]).start()

    def forward(i):
        for s, slot in ((0, 1), (1, 3)):
            whole(gathered.at[slot, i], ag_recv.at[s, i])
            half = pl.ds(s * group, group)
            remote(
                gathered.at[slot, i, half], gathered.at[2, i, half], fw_send.at[s], fw_recv.at[s, i], sides[s]
            ).start()

    def complete(i):
        for s in range(2):
            whole(gathered.at[2, i, pl.ds(s * group, group)], fw_recv.at[s, i])

    def pack(n):
        for rel_y in range(REPS):
            for b in range(2):
                at = n * chunk + (rel_y * 2 + b) * group
                x_rows[at:at + group, :] = gathered[rel_y, 2 * n + b, 0:group, :]
                d_rows[at:at + group, :] = gathered[rel_y, 2 * n + b, group:both, :]

    ff = w_first.shape[1]

    def first_half(n, lo, hi):
        here = pl.ds(n * chunk, chunk)

        @pl.loop(lo, hi)
        def _(t):
            cols = pl.ds(pl.multiple_of(t * tile, tile), tile)
            v = dot(x_rows[here, :], w_first[:, cols])
            g = dot(d_rows[here, :], w_second[cols, :], ((1,), (1,)))
            square = v * v
            th = jnp.tanh(v * (ROOT + (ROOT * CUBIC) * square))
            half_up = 0.5 + 0.5 * th
            hidden[here, cols] = (v * half_up).astype(BF16)
            slope = half_up + (0.5 * v) * (1.0 - th * th) * (ROOT + (3.0 * ROOT * CUBIC) * square)
            d_pre[here, cols] = (g * slope).astype(BF16)

    def second_half(n, lo, hi):
        here = pl.ds(n * chunk, chunk)

        @pl.loop(lo, hi)
        def _(t):
            cols = pl.ds(pl.multiple_of(t * tile, tile), tile)
            y = dot(hidden[here, :], w_second[:, cols]).astype(BF16)
            dx = dot(d_pre[here, :], w_first[cols, :], ((1,), (1,))).astype(BF16)
            for rel_y in range(REPS):
                for b in range(2):
                    at = (rel_y * 2 + b) * group
                    partial[rel_y, 2 * n + b, 0:group, cols] = y[at:at + group]
                    partial[rel_y, 2 * n + b, group:both, cols] = dx[at:at + group]

    opposite = (3, 1)

    def reduce_first(i):
        for s in range(2):
            half = pl.ds(s * group, group)
            other = pl.ds((1 - s) * group, group)
            remote(partial.at[2, i, half], relay.at[s, i], r1_send.at[s], r1_recv.at[s, i], sides[s]).start()
            remote(
                partial.at[opposite[s], i, other], arrived.at[s, i, other], r2_send.at[s], r2_recv.at[s, i], sides[s]
            ).start()

    def reduce_second(i):
        for s in range(2):
            half = pl.ds(s * group, group)
            whole(relay.at[s, i], r1_recv.at[s, i])
            summed = partial[opposite[s], i, half, :].astype(F32) + relay[s, i].astype(F32)
            partial[opposite[s], i, half, :] = summed.astype(BF16)
            remote(
                partial.at[opposite[s], i, half], arrived.at[s, i, half], r2_send.at[s], r2_recv.at[s, i], sides[s]
            ).start()

    def give_back(i):
        for s in range(2):
            whole(arrived.at[s, i], r2_recv.at[s, i])
        summed = partial[0, i].astype(F32) + arrived[0, i].astype(F32) + arrived[1, i].astype(F32)
        back[i] = dot(merge_perm(), summed.astype(BF16)).reshape(plane, UNIT, width).astype(BF16)
        away = order[i]
        if away == 0:
            pltpu.make_async_copy(back.at[i, me_p], returned.at[i, me_p], ret_recv.at[i]).start()

        @pl.loop(1 if away == 0 else 0, plane)
        def _(s):
            p = lax.rem(me_p + s, plane)
            remote(
                back.at[i, p], returned.at[i, me_p], ret_send.at[i], ret_recv.at[i], peer(-away, p)
            ).start()

    def combine(n):
        for b in range(2):
            whole(returned.at[2 * n + b], ret_recv.at[2 * n + b])
        span = 2 * rows_at
        units = returned[2 * n:2 * n + 2].astype(F32).reshape(span, width).astype(BF16)
        got = dot(take[:, n * span:(n + 1) * span], units)
        if n == 0:
            total[...] = got
        else:
            total[...] += got

    stores = []

    def weights_out():
        @pl.loop(0, ff // tile)
        def _(t):
            cols = pl.ds(pl.multiple_of(t * tile, tile), tile)
            g_second[cols, :] = dot(hidden[:, cols], d_rows[...], ((0,), (0,))).astype(BF16)

        stores.append(pltpu.make_async_copy(g_second, grad_out_ref, store_sem.at[1]))
        stores[-1].start()

        @pl.loop(0, width // tile)
        def _(t):
            cols = pl.ds(pl.multiple_of(t * tile, tile), tile)
            g_first[cols, :] = dot(x_rows[:, cols], d_pre[...], ((0,), (0,))).astype(BF16)

        stores.append(pltpu.make_async_copy(g_first, grad_in_ref, store_sem.at[0]))
        stores[-1].start()

    tiles = ff // tile
    for i in range(steps):
        dispatch(i)
    load_first.wait()
    load_second.wait()
    arrive(0)
    arrive(1)
    forward(0)
    forward(1)
    for n in range(chunks):
        last = n == chunks - 1
        if not last:
            arrive(2 * n + 2)
        complete(2 * n)
        complete(2 * n + 1)
        pack(n)
        first_half(n, 0, tiles // 2)
        if not last:
            arrive(2 * n + 3)
        if n:
            reduce_second(2 * n - 2)
            reduce_second(2 * n - 1)
        first_half(n, tiles // 2, tiles)
        if not last:
            forward(2 * n + 2)
        second_half(n, 0, tiles // 2)
        if n:
            give_back(2 * n - 2)
        if not last:
            forward(2 * n + 3)
        second_half(n, tiles // 2, tiles)
        reduce_first(2 * n)
        reduce_first(2 * n + 1)
        if n:
            give_back(2 * n - 1)
    n = chunks - 1
    reduce_second(2 * n)
    reduce_second(2 * n + 1)
    weights_out()
    for i in (2 * n, 2 * n + 1):
        give_back(i)
    for n in range(chunks):
        combine(n)

    picked = total[0:toks, :] * gates_ref[:, 0:1] + total[toks:2 * toks, :] * gates_ref[:, 1:2]
    mixed_ref[...] = (tokens_ref[...].astype(F32) + picked).astype(BF16)
    g = total[2 * toks:3 * toks, :] * gain_ref[...]
    unit = xhat[...]
    inner = g - jnp.mean(g, axis=-1, keepdims=True) - unit * jnp.mean(g * unit, axis=-1, keepdims=True)
    grad_tokens_ref[...] = (cot_ref[...].astype(F32) + scale[...] * inner).astype(BF16)

    for i in range(steps):
        for buf, sem in ((sent, disp_send), (back, ret_send)):
            whole(buf.at[i, 0:plane - 1] if order[i] == 0 else buf.at[i], sem.at[i])
    for s in range(2):
        whole(gathered.at[0], ag_send.at[s])
        whole(gathered.at[0, :, pl.ds(0, group)], fw_send.at[s])
        whole(partial.at[0, :, pl.ds(0, group)], r1_send.at[s])
        whole(partial.at[0], r2_send.at[s])
    for store in stores:
        store.wait()


def local(plane, tokens, gain, expert_ids, gates, w_in, w_out, cotangent):
    experts = lax.axis_size("exp")
    steps = experts // plane
    order = ORDERS[steps]
    toks, width = tokens.shape
    ff = w_in.shape[2]
    group = plane * CAP
    rows = experts * CAP * REPS
    places = experts * UNIT
    dma = pltpu.SemaphoreType.DMA
    vmem = pl.BlockSpec(memory_space=pltpu.VMEM)
    hbm = pl.BlockSpec(memory_space=pl.ANY)
    unit = (steps, plane, UNIT, width)
    mixed, grad_tokens, grad_in, grad_out = pl.pallas_call(
        functools.partial(kernel, order, plane, min(256, ff // 2)),
        out_shape=(
            jax.ShapeDtypeStruct((toks, width), BF16),
            jax.ShapeDtypeStruct((toks, width), BF16),
            jax.ShapeDtypeStruct((width, ff), BF16),
            jax.ShapeDtypeStruct((ff, width), BF16),
        ),
        in_specs=[vmem] * 5 + [hbm] * 2,
        out_specs=(vmem, vmem, hbm, hbm),
        scratch_shapes=[
            pltpu.VMEM((width, ff), BF16),
            pltpu.VMEM((ff, width), BF16),
            pltpu.VMEM(unit, BF16),
            pltpu.VMEM(unit, BF16),
            pltpu.VMEM((REPS, steps, 2 * group, width), BF16),
            pltpu.VMEM((rows, width), BF16),
            pltpu.VMEM((rows, width), BF16),
            pltpu.VMEM((rows, ff), BF16),
            pltpu.VMEM((rows, ff), BF16),
            pltpu.VMEM((REPS, steps, 2 * group, width), BF16),
            pltpu.VMEM((2, steps, group, width), BF16),
            pltpu.VMEM((2, steps, 2 * group, width), BF16),
            pltpu.VMEM(unit, BF16),
            pltpu.VMEM(unit, BF16),
            pltpu.VMEM((places, 3 * toks), BF16),
            pltpu.VMEM((3 * toks, places), BF16),
            pltpu.VMEM((3 * toks, width), BF16),
            pltpu.VMEM((toks, width), F32),
            pltpu.VMEM((toks, 1), F32),
            pltpu.VMEM((3 * toks, width), F32),
            pltpu.VMEM((width, ff), BF16),
            pltpu.VMEM((ff, width), BF16),
            dma((2,)),
            dma((steps,)),
            dma((steps,)),
            dma((2,)),
            dma((2, steps)),
            dma((2,)),
            dma((2, steps)),
            dma((2,)),
            dma((2, steps)),
            dma((2,)),
            dma((2, steps)),
            dma((steps,)),
            dma((steps,)),
            dma((2,)),
        ],
        compiler_params=pltpu.CompilerParams(
            collective_id=0, has_side_effects=True, vmem_limit_bytes=56 * 1024 * 1024
        ),
    )(tokens, gain.reshape(1, width), expert_ids, gates, cotangent, w_in[0], w_out[0])
    return (mixed, grad_tokens, grad_in[None], grad_out[None])


def solution(mesh, plane=PLANE):
    return jax.shard_map(
        functools.partial(local, plane),
        mesh=mesh,
        in_specs=(
            P(("rep", "exp"), None),
            P(),
            P(("rep", "exp"), None),
            P(("rep", "exp"), None),
            P("exp", None, "rep"),
            P("exp", "rep", None),
            P(("rep", "exp"), None),
        ),
        out_specs=(
            P(("rep", "exp"), None),
            P(("rep", "exp"), None),
            P("exp", None, "rep"),
            P("exp", "rep", None),
        ),
        check_vma=False,
    )
```

```python
import functools
import math

import jax
import jax.numpy as jnp
from jax import lax
from jax.experimental import pallas as pl
from jax.experimental.pallas import tpu as pltpu
from jax.sharding import PartitionSpec as P

MESH = pl.DeviceIdType.MESH
F32 = jnp.float32
BF16 = jnp.bfloat16
EPSILON = 1e-05
CAP = 4
UNIT = 2 * CAP
REPS = 4
PLANE = 8
ORDERS = {8: (0, 1, 2, 6, 3, 5, 4, 7), 4: (0, 1, 2, 3), 2: (0, 1)}
ROOT = math.sqrt(2.0 / math.pi)
CUBIC = 0.044715


def dot(left, right, contract=((1,), (0,))):
    return lax.dot_general(left, right, (contract, ((), ())), preferred_element_type=F32)


def kernel(
    order, plane, tile,
    tokens_hbm, gain_ref, ids_ref, gates_ref, cot_hbm, w_in_ref, w_out_ref,
    total, tokens_ref, cot_ref, xhat, scale, columns, g_first, g_second,
    w_first, w_second, sent, landed, gathered, x_rows, d_rows, hidden, d_pre,
    partial, relay, arrived, back, returned, disp, take, rows_in,
    load_sem, disp_send, disp_recv, ag_send, ag_recv, fw_send, fw_recv,
    r1_send, r1_recv, r2_send, r2_recv, ret_send, ret_recv,
):
    steps = len(order)
    toks, width = tokens_ref.shape
    group = plane * CAP
    both = 2 * group
    chunk = 2 * REPS * group
    chunks = steps // 2
    places = steps * plane * UNIT
    me_y = lax.axis_index("rep")
    me_e = lax.axis_index("exp")
    me_z = lax.div(me_e, plane)
    me_p = lax.rem(me_e, plane)
    experts = steps * plane
    up = {"rep": lax.rem(me_y + 1, REPS)}
    down = {"rep": lax.rem(me_y + REPS - 1, REPS)}
    sides = (up, down)

    loads = [
        pltpu.make_async_copy(src, dst, load_sem.at[j])
        for j, (src, dst) in enumerate(
            ((tokens_hbm, tokens_ref), (cot_hbm, cot_ref), (w_in_ref, w_first), (w_out_ref, w_second))
        )
    ]
    loads[0].start()
    loads[1].start()

    barrier = pltpu.get_barrier_semaphore()
    for side in sides:
        pl.semaphore_signal(barrier, inc=1, device_id=side, device_id_type=MESH)

    @pl.loop(1, experts)
    def _(s):
        pl.semaphore_signal(barrier, inc=1, device_id={"exp": lax.rem(me_e + s, experts)}, device_id_type=MESH)

    loads[2].start()
    loads[3].start()

    def place_of(k):
        ids = ids_ref[k:k + 1, :]
        z = lax.rem(lax.div(ids, plane) - me_z + steps, steps)
        position = jnp.zeros_like(z)
        for i, away in enumerate(order):
            position = jnp.where(z == away, i, position)
        return position * plane + lax.rem(ids, plane)

    rel = [place_of(k) for k in range(2)]
    labels = lax.broadcasted_iota(jnp.int32, (experts, toks), 0)
    one = [(labels == r).astype(F32) for r in rel]
    earlier = (
        lax.broadcasted_iota(jnp.int32, (toks, toks), 0) < lax.broadcasted_iota(jnp.int32, (toks, toks), 1)
    ).astype(F32).astype(BF16)
    before = dot((one[0] + one[1]).astype(BF16), earlier)
    targets = []
    for k in range(2):
        rank = jnp.sum(before * one[k], axis=0, keepdims=True).astype(jnp.int32)
        targets.append(jnp.where(rank < CAP, rel[k] * UNIT + rank, -UNIT))
    table = jnp.concatenate(
        [t.astype(F32) for t in targets] + [gates_ref[...], jnp.zeros((4, toks), F32)], axis=0
    ).T
    columns[...] = table
    down_q = lax.broadcasted_iota(jnp.int32, (places, toks), 0)
    disp[:, 0:toks] = ((down_q == targets[0]) | (down_q == targets[1])).astype(F32).astype(BF16)
    for k in range(2):
        disp[:, (k + 1) * toks:(k + 2) * toks] = (down_q == targets[k] + CAP).astype(F32).astype(BF16)

    loads[0].wait()
    values = tokens_ref[...].astype(F32)
    center = values - jnp.mean(values, axis=-1, keepdims=True)
    inv = lax.rsqrt(jnp.mean(center * center, axis=-1, keepdims=True) + EPSILON)
    unit = center * inv
    xhat[...] = unit
    scale[...] = inv
    rows_in[0:toks, :] = (unit * gain_ref[...]).astype(BF16)
    loads[1].wait()
    cot = cot_ref[...].astype(F32)
    for k in range(2):
        rows_in[(k + 1) * toks:(k + 2) * toks, :] = (cot * table[:, 2 + k:3 + k]).astype(BF16)

    def write_take():
        across_q = lax.broadcasted_iota(jnp.int32, (toks, places), 1)
        target = [columns[:, k:k + 1].astype(jnp.int32) for k in range(2)]
        for k in range(2):
            take[k * toks:(k + 1) * toks, :] = (across_q == target[k]).astype(F32).astype(BF16)
        take[2 * toks:3 * toks, :] = (
            (across_q == target[0] + CAP) | (across_q == target[1] + CAP)
        ).astype(F32).astype(BF16)

    def peer(away, p):
        return {"exp": lax.rem(me_z + away + steps, steps) * plane + p}

    rows_at = plane * UNIT

    def dispatch(i):
        piece = dot(disp[i * rows_at:(i + 1) * rows_at, :], rows_in[...])
        sent[i] = piece.reshape(plane, UNIT, width).astype(BF16)
        if i == 0:
            pl.semaphore_wait(barrier, experts - 1 + 2)
        away = order[i]
        if away == 0:
            pltpu.make_async_copy(sent.at[i, me_p], landed.at[i, me_p], disp_recv.at[i]).start()

        @pl.loop(1 if away == 0 else 0, plane)
        def _(s):
            p = lax.rem(me_p + s, plane)
            pltpu.make_async_remote_copy(
                sent.at[i, p], landed.at[i, me_p], disp_send.at[i], disp_recv.at[i],
                device_id=peer(away, p), device_id_type=MESH,
            ).start()

    r = lax.broadcasted_iota(jnp.int32, (both, both), 0)
    c = lax.broadcasted_iota(jnp.int32, (both, both), 1)

    def mixed_row(pure):
        kind = lax.div(pure, group)
        row = lax.rem(pure, group)
        return lax.div(row, CAP) * UNIT + kind * CAP + lax.rem(row, CAP)

    def split_perm():
        return (c == mixed_row(r)).astype(F32).astype(BF16)

    def merge_perm():
        return (r == mixed_row(c)).astype(F32).astype(BF16)

    def whole(ref, sem):
        pltpu.make_async_copy(ref, ref, sem).wait()

    def remote(src, dst, send, recv, where):
        return pltpu.make_async_remote_copy(src, dst, send, recv, device_id=where, device_id_type=MESH)

    def arrive(i):
        whole(landed.at[i], disp_recv.at[i])
        units = landed[i].astype(F32).reshape(both, width).astype(BF16)
        gathered[0, i] = dot(split_perm(), units).astype(BF16)
        for s, slot in ((0, 1), (1, 3)):
            remote(gathered.at[0, i], gathered.at[slot, i], ag_send.at[s], ag_recv.at[s, i], sides[s]).start()

    def forward(i):
        for s, slot in ((0, 1), (1, 3)):
            whole(gathered.at[slot, i], ag_recv.at[s, i])
            half = pl.ds(s * group, group)
            remote(
                gathered.at[slot, i, half], gathered.at[2, i, half], fw_send.at[s], fw_recv.at[s, i], sides[s]
            ).start()

    def complete(i):
        for s in range(2):
            whole(gathered.at[2, i, pl.ds(s * group, group)], fw_recv.at[s, i])

    def pack(n):
        for rel_y in range(REPS):
            for b in range(2):
                at = n * chunk + (rel_y * 2 + b) * group
                x_rows[at:at + group, :] = gathered[rel_y, 2 * n + b, 0:group, :]
                d_rows[at:at + group, :] = gathered[rel_y, 2 * n + b, group:both, :]

    ff = w_first.shape[1]

    def first_half(n, lo, hi):
        here = pl.ds(n * chunk, chunk)

        @pl.loop(lo, hi)
        def _(t):
            cols = pl.ds(pl.multiple_of(t * tile, tile), tile)
            v = dot(x_rows[here, :], w_first[:, cols])
            g = dot(d_rows[here, :], w_second[cols, :], ((1,), (1,)))
            square = v * v
            th = jnp.tanh(v * (ROOT + (ROOT * CUBIC) * square))
            half_up = 0.5 + 0.5 * th
            hidden[here, cols] = (v * half_up).astype(BF16)
            slope = half_up + (0.5 * v) * (1.0 - th * th) * (ROOT + (3.0 * ROOT * CUBIC) * square)
            d_pre[here, cols] = (g * slope).astype(BF16)

    def second_half(n, lo, hi):
        here = pl.ds(n * chunk, chunk)

        @pl.loop(lo, hi)
        def _(t):
            cols = pl.ds(pl.multiple_of(t * tile, tile), tile)
            y = dot(hidden[here, :], w_second[:, cols]).astype(BF16)
            dx = dot(d_pre[here, :], w_first[cols, :], ((1,), (1,))).astype(BF16)
            for rel_y in range(REPS):
                for b in range(2):
                    at = (rel_y * 2 + b) * group
                    partial[rel_y, 2 * n + b, 0:group, cols] = y[at:at + group]
                    partial[rel_y, 2 * n + b, group:both, cols] = dx[at:at + group]

    opposite = (3, 1)

    def reduce_first(group_ids):
        for i in group_ids:
            for s in range(2):
                half = pl.ds(s * group, group)
                remote(partial.at[2, i, half], relay.at[s, i], r1_send.at[s], r1_recv.at[s, i], sides[s]).start()
        for i in group_ids:
            for s in range(2):
                half = pl.ds((1 - s) * group, group)
                remote(
                    partial.at[opposite[s], i, half], arrived.at[s, i, half], r2_send.at[s], r2_recv.at[s, i], sides[s]
                ).start()

    def reduce_second(i):
        for s in range(2):
            half = pl.ds(s * group, group)
            whole(relay.at[s, i], r1_recv.at[s, i])
            summed = partial[opposite[s], i, half, :].astype(F32) + relay[s, i].astype(F32)
            partial[opposite[s], i, half, :] = summed.astype(BF16)
            remote(
                partial.at[opposite[s], i, half], arrived.at[s, i, half], r2_send.at[s], r2_recv.at[s, i], sides[s]
            ).start()

    def give_back(i):
        for s in range(2):
            whole(arrived.at[s, i], r2_recv.at[s, i])
        summed = partial[0, i].astype(F32) + arrived[0, i].astype(F32) + arrived[1, i].astype(F32)
        back[i] = dot(merge_perm(), summed.astype(BF16)).reshape(plane, UNIT, width).astype(BF16)
        away = order[i]
        if away == 0:
            pltpu.make_async_copy(back.at[i, me_p], returned.at[i, me_p], ret_recv.at[i]).start()

        @pl.loop(1 if away == 0 else 0, plane)
        def _(s):
            p = lax.rem(me_p + s, plane)
            remote(
                back.at[i, p], returned.at[i, me_p], ret_send.at[i], ret_recv.at[i], peer(-away, p)
            ).start()

    def combine(n):
        for b in range(2):
            whole(returned.at[2 * n + b], ret_recv.at[2 * n + b])
        span = 2 * rows_at
        units = returned[2 * n:2 * n + 2].astype(F32).reshape(span, width).astype(BF16)
        got = dot(take[:, n * span:(n + 1) * span], units)
        if n == 0:
            total[...] = got
        else:
            total[...] += got

    def out_grad(lo, hi):
        @pl.loop(lo, hi)
        def _(t):
            cols = pl.ds(pl.multiple_of(t * tile, tile), tile)
            g_second[cols, :] = dot(hidden[:, cols], d_rows[...], ((0,), (0,))).astype(BF16)

    def in_grad(lo, hi):
        @pl.loop(lo, hi)
        def _(t):
            cols = pl.ds(pl.multiple_of(t * tile, tile), tile)
            g_first[cols, :] = dot(x_rows[:, cols], d_pre[...], ((0,), (0,))).astype(BF16)

    tiles = ff // tile
    cut = tiles // 2
    ready = iter(range(steps))
    passed = iter(range(steps))

    def arrive_next():
        i = next(ready, None)
        if i is not None:
            arrive(i)

    def forward_next():
        i = next(passed, None)
        if i is not None:
            forward(i)

    early = min(4, steps)
    dispatch(0)
    dispatch(1)
    arrive_next()
    for i in range(2, early):
        dispatch(i)
    arrive_next()
    for i in range(early, steps):
        dispatch(i)
    forward_next()
    arrive_next()
    write_take()
    forward_next()
    arrive_next()
    loads[2].wait()
    loads[3].wait()
    for n in range(chunks):
        complete(2 * n)
        complete(2 * n + 1)
        pack(n)
        first_half(n, 0, cut)
        forward_next()
        if n:
            reduce_second(2 * n - 2)
        first_half(n, cut, tiles)
        arrive_next()
        forward_next()
        if n:
            reduce_second(2 * n - 1)
        second_half(n, 0, cut)
        arrive_next()
        second_half(n, cut, tiles)
        reduce_first((2 * n, 2 * n + 1))
        if n:
            give_back(2 * n - 2)
            give_back(2 * n - 1)
    n = chunks - 1
    out_grad(0, cut)
    reduce_second(2 * n)
    out_grad(cut, tiles)
    reduce_second(2 * n + 1)
    in_grad(0, cut)
    give_back(2 * n)
    in_grad(cut, tiles)
    give_back(2 * n + 1)
    for n in range(chunks):
        combine(n)

    for i in range(steps):
        for buf, sem in ((sent, disp_send), (back, ret_send)):
            whole(buf.at[i, 0:plane - 1] if order[i] == 0 else buf.at[i], sem.at[i])
    for s in range(2):
        whole(gathered.at[0], ag_send.at[s])
        whole(gathered.at[0, :, pl.ds(0, group)], fw_send.at[s])
        whole(partial.at[0, :, pl.ds(0, group)], r1_send.at[s])
        whole(partial.at[0], r2_send.at[s])


def finish(
    total, tokens_ref, cot_ref, xhat, scale, columns, g_first, g_second, gain_ref,
    mixed_ref, grad_tokens_ref, grad_in_ref, grad_out_ref, mixed, grad_tokens, store_sem,
):
    toks = tokens_ref.shape[0]
    stores = [
        pltpu.make_async_copy(src, dst, store_sem.at[j])
        for j, (src, dst) in enumerate((
            (g_first, grad_in_ref), (g_second, grad_out_ref), (mixed, mixed_ref), (grad_tokens, grad_tokens_ref),
        ))
    ]
    stores[0].start()
    stores[1].start()
    picked = total[0:toks, :] * columns[:, 2:3] + total[toks:2 * toks, :] * columns[:, 3:4]
    mixed[...] = (tokens_ref[...].astype(F32) + picked).astype(BF16)
    stores[2].start()
    g = total[2 * toks:3 * toks, :] * gain_ref[...]
    unit = xhat[...]
    inner = g - jnp.mean(g, axis=-1, keepdims=True) - unit * jnp.mean(g * unit, axis=-1, keepdims=True)
    grad_tokens[...] = (cot_ref[...].astype(F32) + scale[...] * inner).astype(BF16)
    stores[3].start()
    for store in stores:
        store.wait()


def local(plane, tokens, gain, expert_ids, gates, w_in, w_out, cotangent):
    experts = lax.axis_size("exp")
    steps = experts // plane
    order = ORDERS[steps]
    toks, width = tokens.shape
    ff = w_in.shape[2]
    group = plane * CAP
    rows = experts * CAP * REPS
    places = experts * UNIT
    dma = pltpu.SemaphoreType.DMA
    vmem = pl.BlockSpec(memory_space=pltpu.VMEM)
    hbm = pl.BlockSpec(memory_space=pl.ANY)
    unit = (steps, plane, UNIT, width)
    held = pl.pallas_call(
        functools.partial(kernel, order, plane, min(256, ff // 2)),
        out_shape=(
            pltpu.VMEM((3 * toks, width), F32),
            pltpu.VMEM((toks, width), BF16),
            pltpu.VMEM((toks, width), BF16),
            pltpu.VMEM((toks, width), F32),
            pltpu.VMEM((toks, 1), F32),
            pltpu.VMEM((toks, 8), F32),
            pltpu.VMEM((width, ff), BF16),
            pltpu.VMEM((ff, width), BF16),
        ),
        in_specs=[hbm, vmem, vmem, vmem, hbm, hbm, hbm],
        out_specs=(vmem,) * 8,
        scratch_shapes=[
            pltpu.VMEM((width, ff), BF16),
            pltpu.VMEM((ff, width), BF16),
            pltpu.VMEM(unit, BF16),
            pltpu.VMEM(unit, BF16),
            pltpu.VMEM((REPS, steps, 2 * group, width), BF16),
            pltpu.VMEM((rows, width), BF16),
            pltpu.VMEM((rows, width), BF16),
            pltpu.VMEM((rows, ff), BF16),
            pltpu.VMEM((rows, ff), BF16),
            pltpu.VMEM((REPS, steps, 2 * group, width), BF16),
            pltpu.VMEM((2, steps, group, width), BF16),
            pltpu.VMEM((2, steps, 2 * group, width), BF16),
            pltpu.VMEM(unit, BF16),
            pltpu.VMEM(unit, BF16),
            pltpu.VMEM((places, 3 * toks), BF16),
            pltpu.VMEM((3 * toks, places), BF16),
            pltpu.VMEM((3 * toks, width), BF16),
            dma((4,)),
            dma((steps,)),
            dma((steps,)),
            dma((2,)),
            dma((2, steps)),
            dma((2,)),
            dma((2, steps)),
            dma((2,)),
            dma((2, steps)),
            dma((2,)),
            dma((2, steps)),
            dma((steps,)),
            dma((steps,)),
        ],
        compiler_params=pltpu.CompilerParams(
            collective_id=0, has_side_effects=True, vmem_limit_bytes=53 * 1024 * 1024
        ),
    )(tokens, gain.reshape(1, width), expert_ids.T, gates.T, cotangent, w_in[0], w_out[0])
    mixed, grad_tokens, grad_in, grad_out = pl.pallas_call(
        finish,
        out_shape=(
            jax.ShapeDtypeStruct((toks, width), BF16),
            jax.ShapeDtypeStruct((toks, width), BF16),
            jax.ShapeDtypeStruct((width, ff), BF16),
            jax.ShapeDtypeStruct((ff, width), BF16),
        ),
        in_specs=[vmem] * 9,
        out_specs=(hbm,) * 4,
        scratch_shapes=[
            pltpu.VMEM((toks, width), BF16),
            pltpu.VMEM((toks, width), BF16),
            dma((4,)),
        ],
        compiler_params=pltpu.CompilerParams(vmem_limit_bytes=16 * 1024 * 1024),
    )(*[pltpu.with_memory_space_constraint(h, pltpu.VMEM) for h in held], gain.reshape(1, width))
    return (mixed, grad_tokens, grad_in[None], grad_out[None])


def solution(mesh, plane=PLANE):
    return jax.shard_map(
        functools.partial(local, plane),
        mesh=mesh,
        in_specs=(
            P(("rep", "exp"), None),
            P(),
            P(("rep", "exp"), None),
            P(("rep", "exp"), None),
            P("exp", None, "rep"),
            P("exp", "rep", None),
            P(("rep", "exp"), None),
        ),
        out_specs=(
            P(("rep", "exp"), None),
            P(("rep", "exp"), None),
            P("exp", None, "rep"),
            P("exp", "rep", None),
        ),
        check_vma=False,
    )
```

```python
import functools
import math

import jax
import jax.numpy as jnp
from jax import lax
from jax.experimental import pallas as pl
from jax.experimental.pallas import tpu as pltpu
from jax.sharding import PartitionSpec as P

MESH = pl.DeviceIdType.MESH
F32 = jnp.float32
BF16 = jnp.bfloat16
EPSILON = 1e-05
CAP = 4
UNIT = 2 * CAP
REPS = 4
PLANE = 8
ORDERS = {8: (0, 1, 6, 2, 5, 3, 4, 7), 4: (0, 1, 2, 3)}
FIRST = (0, -1)
LATE = (0, 1)
ROOT = math.sqrt(2.0 / math.pi)
CUBIC = 0.044715


def places_of(which, steps):
    return tuple(i % steps for i in which)


def dot(left, right, contract=((1,), (0,))):
    return lax.dot_general(left, right, (contract, ((), ())), preferred_element_type=F32)


def kernel(
    order, plane, tile,
    tokens_hbm, gain_ref, ids_ref, gates_ref, cot_hbm, w_in_ref, w_out_ref,
    total, tokens_ref, cot_ref, xhat, scale, columns, g_first, g_second,
    w_first, w_second, sent, landed, gathered, x_rows, d_rows, hidden, d_pre,
    partial, relay, arrived, back, returned, disp, take, rows_in,
    early, spread_in, late_out, home, home_relay, home_in,
    load_sem, disp_send, disp_recv, ag_send, ag_recv, fw_send, fw_recv,
    r1_send, r1_recv, r2_send, r2_recv, ret_send, ret_recv, sp_send, sp_recv, lt_send, lt_recv,
):
    steps = len(order)
    toks, width = tokens_ref.shape
    group = plane * CAP
    both = 2 * group
    chunk = 2 * REPS * group
    chunks = steps // 2
    first = places_of(FIRST, steps)
    lates = places_of(LATE, steps)
    places = steps * plane * UNIT
    me_y = lax.axis_index("rep")
    me_e = lax.axis_index("exp")
    me_z = lax.div(me_e, plane)
    me_p = lax.rem(me_e, plane)
    experts = steps * plane
    up = {"rep": lax.rem(me_y + 1, REPS)}
    down = {"rep": lax.rem(me_y + REPS - 1, REPS)}
    sides = (up, down)

    loads = [
        pltpu.make_async_copy(src, dst, load_sem.at[j])
        for j, (src, dst) in enumerate(
            ((tokens_hbm, tokens_ref), (cot_hbm, cot_ref), (w_in_ref, w_first), (w_out_ref, w_second))
        )
    ]
    loads[0].start()
    loads[1].start()

    barrier = pltpu.get_barrier_semaphore()
    for side in sides:
        pl.semaphore_signal(barrier, inc=1, device_id=side, device_id_type=MESH)

    @pl.loop(1, experts)
    def _(s):
        pl.semaphore_signal(barrier, inc=1, device_id={"exp": lax.rem(me_e + s, experts)}, device_id_type=MESH)

    loads[2].start()
    loads[3].start()

    def place_of(k):
        ids = ids_ref[k:k + 1, :]
        z = lax.rem(lax.div(ids, plane) - me_z + steps, steps)
        position = jnp.zeros_like(z)
        for i, away in enumerate(order):
            position = jnp.where(z == away, i, position)
        return position * plane + lax.rem(ids, plane)

    rel = [place_of(k) for k in range(2)]
    labels = lax.broadcasted_iota(jnp.int32, (experts, toks), 0)
    one = [(labels == r).astype(F32) for r in rel]
    earlier = (
        lax.broadcasted_iota(jnp.int32, (toks, toks), 0) < lax.broadcasted_iota(jnp.int32, (toks, toks), 1)
    ).astype(F32).astype(BF16)
    before = dot((one[0] + one[1]).astype(BF16), earlier)
    targets = []
    for k in range(2):
        rank = jnp.sum(before * one[k], axis=0, keepdims=True).astype(jnp.int32)
        targets.append(jnp.where(rank < CAP, rel[k] * UNIT + rank, -UNIT))
    table = jnp.concatenate(
        [t.astype(F32) for t in targets] + [gates_ref[...], jnp.zeros((4, toks), F32)], axis=0
    ).T
    columns[...] = table
    down_q = lax.broadcasted_iota(jnp.int32, (places, toks), 0)
    disp[:, 0:toks] = ((down_q == targets[0]) | (down_q == targets[1])).astype(F32).astype(BF16)
    for k in range(2):
        disp[:, (k + 1) * toks:(k + 2) * toks] = (down_q == targets[k] + CAP).astype(F32).astype(BF16)

    loads[0].wait()
    values = tokens_ref[...].astype(F32)
    center = values - jnp.mean(values, axis=-1, keepdims=True)
    inv = lax.rsqrt(jnp.mean(center * center, axis=-1, keepdims=True) + EPSILON)
    unit = center * inv
    xhat[...] = unit
    scale[...] = inv
    rows_in[0:toks, :] = (unit * gain_ref[...]).astype(BF16)
    loads[1].wait()
    cot = cot_ref[...].astype(F32)
    for k in range(2):
        rows_in[(k + 1) * toks:(k + 2) * toks, :] = (cot * table[:, 2 + k:3 + k]).astype(BF16)

    def write_take():
        across_q = lax.broadcasted_iota(jnp.int32, (toks, places), 1)
        target = [columns[:, k:k + 1].astype(jnp.int32) for k in range(2)]
        for k in range(2):
            take[k * toks:(k + 1) * toks, :] = (across_q == target[k]).astype(F32).astype(BF16)
        take[2 * toks:3 * toks, :] = (
            (across_q == target[0] + CAP) | (across_q == target[1] + CAP)
        ).astype(F32).astype(BF16)

    def peer(away, p):
        return {"exp": lax.rem(me_z + away + steps, steps) * plane + p}

    rows_at = plane * UNIT

    def dispatch(i):
        piece = dot(disp[i * rows_at:(i + 1) * rows_at, :], rows_in[...])
        piece = piece.reshape(plane, UNIT, width).astype(BF16)
        if i in first:
            early[first.index(i), 0] = piece
        else:
            sent[i] = piece
        if i == 0:
            pl.semaphore_wait(barrier, experts - 1 + 2)
        away = order[i]
        if i in first:
            f = first.index(i)
            for s, slot in ((0, 1), (1, 3)):
                remote(early.at[f, 0], early.at[f, slot], ag_send.at[s], ag_recv.at[s, i], sides[s]).start()
            if i == 0:
                spread(i, 0)
            return
        if away == 0:
            pltpu.make_async_copy(sent.at[i, me_p], landed.at[i, me_p], disp_recv.at[i]).start()

        @pl.loop(1 if away == 0 else 0, plane)
        def _(s):
            p = lax.rem(me_p + s, plane)
            pltpu.make_async_remote_copy(
                sent.at[i, p], landed.at[i, me_p], disp_send.at[i], disp_recv.at[i],
                device_id=peer(away, p), device_id_type=MESH,
            ).start()

    r = lax.broadcasted_iota(jnp.int32, (both, both), 0)
    c = lax.broadcasted_iota(jnp.int32, (both, both), 1)

    def mixed_row(pure):
        kind = lax.div(pure, group)
        row = lax.rem(pure, group)
        return lax.div(row, CAP) * UNIT + kind * CAP + lax.rem(row, CAP)

    def split_perm():
        return (c == mixed_row(r)).astype(F32).astype(BF16)

    def merge_perm():
        return (r == mixed_row(c)).astype(F32).astype(BF16)

    def whole(ref, sem):
        pltpu.make_async_copy(ref, ref, sem).wait()

    def remote(src, dst, send, recv, where):
        return pltpu.make_async_remote_copy(src, dst, send, recv, device_id=where, device_id_type=MESH)

    def arrive(i):
        whole(landed.at[i], disp_recv.at[i])
        units = landed[i].astype(F32).reshape(both, width).astype(BF16)
        gathered[0, i] = dot(split_perm(), units).astype(BF16)
        for s, slot in ((0, 1), (1, 3)):
            remote(gathered.at[0, i], gathered.at[slot, i], ag_send.at[s], ag_recv.at[s, i], sides[s]).start()

    def fan(src, dst, send, recv, away):
        if away == 0:
            pltpu.make_async_copy(src.at[me_p], dst.at[me_p], recv).start()

        @pl.loop(1 if away == 0 else 0, plane)
        def _(s):
            p = lax.rem(me_p + s, plane)
            remote(src.at[p], dst.at[me_p], send, recv, peer(away, p)).start()

    def spread(i, slot):
        f = first.index(i)
        fan(early.at[f, slot], spread_in.at[f, slot], sp_send.at[f, slot], sp_recv.at[f, slot], order[i])

    def forward_early(i):
        f = first.index(i)
        for s, slot in ((0, 1), (1, 3)):
            whole(early.at[f, slot], ag_recv.at[s, i])
            half = pl.ds(s * (plane // 2), plane // 2)
            remote(
                early.at[f, slot, half], early.at[f, 2, half], fw_send.at[s], fw_recv.at[s, i], sides[s]
            ).start()
        if i == 0:
            for slot in (1, 3):
                spread(i, slot)

    def complete_early(i):
        f = first.index(i)
        for s in range(2):
            whole(early.at[f, 2, pl.ds(s * (plane // 2), plane // 2)], fw_recv.at[s, i])
        for slot in ((2,) if i == 0 else (0, 1, 3, 2)):
            spread(i, slot)

    def landed_early(i):
        f = first.index(i)
        for slot in (0, 1, 3, 2):
            whole(spread_in.at[f, slot], sp_recv.at[f, slot])
            units = spread_in[f, slot].astype(F32).reshape(both, width).astype(BF16)
            gathered[slot, i] = dot(split_perm(), units).astype(BF16)

    def forward(i):
        for s, slot in ((0, 1), (1, 3)):
            whole(gathered.at[slot, i], ag_recv.at[s, i])
            half = pl.ds(s * group, group)
            remote(
                gathered.at[slot, i, half], gathered.at[2, i, half], fw_send.at[s], fw_recv.at[s, i], sides[s]
            ).start()

    def complete(i):
        if i in first:
            landed_early(i)
            return
        for s in range(2):
            whole(gathered.at[2, i, pl.ds(s * group, group)], fw_recv.at[s, i])

    def pack(n):
        for rel_y in range(REPS):
            for b in range(2):
                at = n * chunk + (rel_y * 2 + b) * group
                x_rows[at:at + group, :] = gathered[rel_y, 2 * n + b, 0:group, :]
                d_rows[at:at + group, :] = gathered[rel_y, 2 * n + b, group:both, :]

    ff = w_first.shape[1]

    def first_half(n, lo, hi):
        here = pl.ds(n * chunk, chunk)

        @pl.loop(lo, hi)
        def _(t):
            cols = pl.ds(pl.multiple_of(t * tile, tile), tile)
            v = dot(x_rows[here, :], w_first[:, cols])
            g = dot(d_rows[here, :], w_second[cols, :], ((1,), (1,)))
            square = v * v
            th = jnp.tanh(v * (ROOT + (ROOT * CUBIC) * square))
            half_up = 0.5 + 0.5 * th
            hidden[here, cols] = (v * half_up).astype(BF16)
            slope = half_up + (0.5 * v) * (1.0 - th * th) * (ROOT + (3.0 * ROOT * CUBIC) * square)
            d_pre[here, cols] = (g * slope).astype(BF16)

    def second_half(n, lo, hi):
        here = pl.ds(n * chunk, chunk)

        @pl.loop(lo, hi)
        def _(t):
            cols = pl.ds(pl.multiple_of(t * tile, tile), tile)
            y = dot(hidden[here, :], w_second[:, cols]).astype(BF16)
            dx = dot(d_pre[here, :], w_first[cols, :], ((1,), (1,))).astype(BF16)
            for rel_y in range(REPS):
                for b in range(2):
                    at = (rel_y * 2 + b) * group
                    partial[rel_y, 2 * n + b, 0:group, cols] = y[at:at + group]
                    partial[rel_y, 2 * n + b, group:both, cols] = dx[at:at + group]

    opposite = (3, 1)

    def reduce_first(group_ids):
        for i in group_ids:
            for s in range(2):
                half = pl.ds(s * group, group)
                remote(partial.at[2, i, half], relay.at[s, i], r1_send.at[s], r1_recv.at[s, i], sides[s]).start()
        for i in group_ids:
            for s in range(2):
                half = pl.ds((1 - s) * group, group)
                remote(
                    partial.at[opposite[s], i, half], arrived.at[s, i, half], r2_send.at[s], r2_recv.at[s, i], sides[s]
                ).start()

    def reduce_second(i):
        for s in range(2):
            half = pl.ds(s * group, group)
            whole(relay.at[s, i], r1_recv.at[s, i])
            summed = partial[opposite[s], i, half, :].astype(F32) + relay[s, i].astype(F32)
            partial[opposite[s], i, half, :] = summed.astype(BF16)
            remote(
                partial.at[opposite[s], i, half], arrived.at[s, i, half], r2_send.at[s], r2_recv.at[s, i], sides[s]
            ).start()

    def give_back(i):
        for s in range(2):
            whole(arrived.at[s, i], r2_recv.at[s, i])
        summed = partial[0, i].astype(F32) + arrived[0, i].astype(F32) + arrived[1, i].astype(F32)
        back[i] = dot(merge_perm(), summed.astype(BF16)).reshape(plane, UNIT, width).astype(BF16)
        away = order[i]
        if away == 0:
            pltpu.make_async_copy(back.at[i, me_p], returned.at[i, me_p], ret_recv.at[i]).start()

        @pl.loop(1 if away == 0 else 0, plane)
        def _(s):
            p = lax.rem(me_p + s, plane)
            remote(
                back.at[i, p], returned.at[i, me_p], ret_send.at[i], ret_recv.at[i], peer(-away, p)
            ).start()

    def late_send(i):
        l = lates.index(i)
        for slot in (2, 3, 1, 0):
            late_out[l, slot] = dot(merge_perm(), partial[slot, i]).reshape(plane, UNIT, width).astype(BF16)
            fan(late_out.at[l, slot], home.at[l, slot], lt_send.at[l, slot], lt_recv.at[l, slot], -order[i])

    def late_first(i):
        l = lates.index(i)
        whole(home.at[l, 2], lt_recv.at[l, 2])
        for s in range(2):
            half = pl.ds(s * (plane // 2), plane // 2)
            remote(home.at[l, 2, half], home_relay.at[l, s], r1_send.at[s], r1_recv.at[s, i], sides[s]).start()
        for s in range(2):
            whole(home.at[l, opposite[s]], lt_recv.at[l, opposite[s]])
            half = pl.ds((1 - s) * (plane // 2), plane // 2)
            remote(
                home.at[l, opposite[s], half], home_in.at[l, s, half], r2_send.at[s], r2_recv.at[s, i], sides[s]
            ).start()

    def late_second(i):
        l = lates.index(i)
        for s in range(2):
            half = pl.ds(s * (plane // 2), plane // 2)
            whole(home_relay.at[l, s], r1_recv.at[s, i])
            summed = home[l, opposite[s], half].astype(F32) + home_relay[l, s].astype(F32)
            home[l, opposite[s], half] = summed.astype(BF16)
            remote(
                home.at[l, opposite[s], half], home_in.at[l, s, half], r2_send.at[s], r2_recv.at[s, i], sides[s]
            ).start()

    def late_third(i):
        l = lates.index(i)
        whole(home.at[l, 0], lt_recv.at[l, 0])
        for s in range(2):
            whole(home_in.at[l, s], r2_recv.at[s, i])
        summed = home[l, 0].astype(F32) + home_in[l, 0].astype(F32) + home_in[l, 1].astype(F32)
        returned[i] = summed.astype(BF16)

    def combine(n, start):
        for b in range(2):
            if 2 * n + b in lates:
                late_third(2 * n + b)
                continue
            whole(returned.at[2 * n + b], ret_recv.at[2 * n + b])
        span = 2 * rows_at
        units = returned[2 * n:2 * n + 2].astype(F32).reshape(span, width).astype(BF16)
        got = dot(take[:, n * span:(n + 1) * span], units)
        if start:
            total[...] = got
        else:
            total[...] += got

    def out_grad(lo, hi):
        @pl.loop(lo, hi)
        def _(t):
            cols = pl.ds(pl.multiple_of(t * tile, tile), tile)
            g_second[cols, :] = dot(hidden[:, cols], d_rows[...], ((0,), (0,))).astype(BF16)

    def in_grad(lo, hi):
        @pl.loop(lo, hi)
        def _(t):
            cols = pl.ds(pl.multiple_of(t * tile, tile), tile)
            g_first[cols, :] = dot(x_rows[:, cols], d_pre[...], ((0,), (0,))).astype(BF16)

    tiles = ff // tile
    cut = tiles // 2
    normal = [i for i in range(steps) if i not in first]
    ready = iter(normal)
    passed = iter(normal)

    def arrive_next():
        i = next(ready, None)
        if i is not None:
            arrive(i)

    def forward_next():
        i = next(passed, None)
        if i is not None:
            forward(i)

    for i in first:
        dispatch(i)
    for i in normal[:4]:
        dispatch(i)
    write_take()
    forward_early(0)
    for i in normal[4:]:
        dispatch(i)
    arrive_next()
    for i in first[1:]:
        forward_early(i)
    complete_early(0)
    arrive_next()
    forward_next()
    arrive_next()
    for i in first[1:]:
        complete_early(i)
    loads[2].wait()
    loads[3].wait()
    for n in range(chunks):
        pair = (2 * n, 2 * n + 1)
        late = [i for i in pair if i in lates]
        soon = [i for i in pair if i not in lates]
        before = [i for i in (2 * n - 2, 2 * n - 1) if i >= 0 and i not in lates]
        if n == 0:
            forward_next()
        complete(2 * n)
        complete(2 * n + 1)
        pack(n)
        first_half(n, 0, cut)
        arrive_next()
        for i in before[:1]:
            reduce_second(i)
        first_half(n, cut, tiles)
        forward_next()
        for i in before[1:]:
            reduce_second(i)
        second_half(n, 0, cut)
        arrive_next()
        second_half(n, cut, tiles)
        reduce_first(soon)
        for i in late:
            late_send(i)
        forward_next()
        if n == chunks - 1:
            out_grad(0, cut)
        for i in before:
            give_back(i)
    out_grad(cut, tiles)
    for i in (steps - 2, steps - 1):
        reduce_second(i)
    for i in lates:
        late_first(i)
    in_grad(0, cut)
    for i in (steps - 2, steps - 1):
        give_back(i)
    for i in lates:
        late_second(i)
    in_grad(cut, tiles)
    finals = sorted(range(chunks), key=lambda n: (2 * n in lates or 2 * n + 1 in lates, n))
    for n in finals:
        combine(n, n == finals[0])

    for i in range(steps):
        for buf, sem, other in ((sent, disp_send, first), (back, ret_send, lates)):
            if i in other:
                continue
            whole(buf.at[i, 0:plane - 1] if order[i] == 0 else buf.at[i], sem.at[i])
    for buf, sem, which in ((early, sp_send, first), (late_out, lt_send, lates)):
        for j, i in enumerate(which):
            for slot in range(REPS):
                whole(buf.at[j, slot, 0:plane - 1] if order[i] == 0 else buf.at[j, slot], sem.at[j, slot])
    for s in range(2):
        whole(gathered.at[0], ag_send.at[s])
        whole(gathered.at[0, :, pl.ds(0, group)], fw_send.at[s])
        whole(partial.at[0, :, pl.ds(0, group)], r1_send.at[s])
        whole(partial.at[0], r2_send.at[s])


def finish(
    total, tokens_ref, cot_ref, xhat, scale, columns, g_first, g_second, gain_ref,
    mixed_ref, grad_tokens_ref, grad_in_ref, grad_out_ref, mixed, grad_tokens, store_sem,
):
    toks = tokens_ref.shape[0]
    stores = [
        pltpu.make_async_copy(src, dst, store_sem.at[j])
        for j, (src, dst) in enumerate((
            (g_first, grad_in_ref), (g_second, grad_out_ref), (mixed, mixed_ref), (grad_tokens, grad_tokens_ref),
        ))
    ]
    stores[0].start()
    stores[1].start()
    picked = total[0:toks, :] * columns[:, 2:3] + total[toks:2 * toks, :] * columns[:, 3:4]
    mixed[...] = (tokens_ref[...].astype(F32) + picked).astype(BF16)
    stores[2].start()
    g = total[2 * toks:3 * toks, :] * gain_ref[...]
    unit = xhat[...]
    inner = g - jnp.mean(g, axis=-1, keepdims=True) - unit * jnp.mean(g * unit, axis=-1, keepdims=True)
    grad_tokens[...] = (cot_ref[...].astype(F32) + scale[...] * inner).astype(BF16)
    stores[3].start()
    for store in stores:
        store.wait()


def local(plane, tokens, gain, expert_ids, gates, w_in, w_out, cotangent):
    experts = lax.axis_size("exp")
    steps = experts // plane
    order = ORDERS[steps]
    toks, width = tokens.shape
    ff = w_in.shape[2]
    group = plane * CAP
    rows = experts * CAP * REPS
    places = experts * UNIT
    dma = pltpu.SemaphoreType.DMA
    vmem = pl.BlockSpec(memory_space=pltpu.VMEM)
    hbm = pl.BlockSpec(memory_space=pl.ANY)
    unit = (steps, plane, UNIT, width)
    held = pl.pallas_call(
        functools.partial(kernel, order, plane, min(256, ff // 2)),
        out_shape=(
            pltpu.VMEM((3 * toks, width), F32),
            pltpu.VMEM((toks, width), BF16),
            pltpu.VMEM((toks, width), BF16),
            pltpu.VMEM((toks, width), F32),
            pltpu.VMEM((toks, 1), F32),
            pltpu.VMEM((toks, 8), F32),
            pltpu.VMEM((width, ff), BF16),
            pltpu.VMEM((ff, width), BF16),
        ),
        in_specs=[hbm, vmem, vmem, vmem, hbm, hbm, hbm],
        out_specs=(vmem,) * 8,
        scratch_shapes=[
            pltpu.VMEM((width, ff), BF16),
            pltpu.VMEM((ff, width), BF16),
            pltpu.VMEM(unit, BF16),
            pltpu.VMEM(unit, BF16),
            pltpu.VMEM((REPS, steps, 2 * group, width), BF16),
            pltpu.VMEM((rows, width), BF16),
            pltpu.VMEM((rows, width), BF16),
            pltpu.VMEM((rows, ff), BF16),
            pltpu.VMEM((rows, ff), BF16),
            pltpu.VMEM((REPS, steps, 2 * group, width), BF16),
            pltpu.VMEM((2, steps, group, width), BF16),
            pltpu.VMEM((2, steps, 2 * group, width), BF16),
            pltpu.VMEM(unit, BF16),
            pltpu.VMEM(unit, BF16),
            pltpu.VMEM((places, 3 * toks), BF16),
            pltpu.VMEM((3 * toks, places), BF16),
            pltpu.VMEM((3 * toks, width), BF16),
            pltpu.VMEM((len(FIRST), REPS) + unit[1:], BF16),
            pltpu.VMEM((len(FIRST), REPS) + unit[1:], BF16),
            pltpu.VMEM((len(LATE), REPS) + unit[1:], BF16),
            pltpu.VMEM((len(LATE), REPS) + unit[1:], BF16),
            pltpu.VMEM((len(LATE), 2, plane // 2, UNIT, width), BF16),
            pltpu.VMEM((len(LATE), 2) + unit[1:], BF16),
            dma((4,)),
            dma((steps,)),
            dma((steps,)),
            dma((2,)),
            dma((2, steps)),
            dma((2,)),
            dma((2, steps)),
            dma((2,)),
            dma((2, steps)),
            dma((2,)),
            dma((2, steps)),
            dma((steps,)),
            dma((steps,)),
            dma((len(FIRST), REPS)),
            dma((len(FIRST), REPS)),
            dma((len(LATE), REPS)),
            dma((len(LATE), REPS)),
        ],
        compiler_params=pltpu.CompilerParams(
            collective_id=0, has_side_effects=True, vmem_limit_bytes=53 * 1024 * 1024
        ),
    )(tokens, gain.reshape(1, width), expert_ids.T, gates.T, cotangent, w_in[0], w_out[0])
    mixed, grad_tokens, grad_in, grad_out = pl.pallas_call(
        finish,
        out_shape=(
            jax.ShapeDtypeStruct((toks, width), BF16),
            jax.ShapeDtypeStruct((toks, width), BF16),
            jax.ShapeDtypeStruct((width, ff), BF16),
            jax.ShapeDtypeStruct((ff, width), BF16),
        ),
        in_specs=[vmem] * 9,
        out_specs=(hbm,) * 4,
        scratch_shapes=[
            pltpu.VMEM((toks, width), BF16),
            pltpu.VMEM((toks, width), BF16),
            dma((4,)),
        ],
        compiler_params=pltpu.CompilerParams(vmem_limit_bytes=16 * 1024 * 1024),
    )(*[pltpu.with_memory_space_constraint(h, pltpu.VMEM) for h in held], gain.reshape(1, width))
    return (mixed, grad_tokens, grad_in[None], grad_out[None])


def solution(mesh, plane=PLANE):
    return jax.shard_map(
        functools.partial(local, plane),
        mesh=mesh,
        in_specs=(
            P(("rep", "exp"), None),
            P(),
            P(("rep", "exp"), None),
            P(("rep", "exp"), None),
            P("exp", None, "rep"),
            P("exp", "rep", None),
            P(("rep", "exp"), None),
        ),
        out_specs=(
            P(("rep", "exp"), None),
            P(("rep", "exp"), None),
            P("exp", None, "rep"),
            P("exp", "rep", None),
        ),
        check_vma=False,
    )
```

```python
import functools
import math

import jax
import jax.numpy as jnp
from jax import lax
from jax.experimental import pallas as pl
from jax.experimental.pallas import tpu as pltpu
from jax.sharding import PartitionSpec as P

MESH = pl.DeviceIdType.MESH
F32 = jnp.float32
BF16 = jnp.bfloat16
EPSILON = 1e-05
CAP = 4
UNIT = 2 * CAP
REPS = 4
PLANE = 8
ORDERS = {8: (0, 1, 6, 2, 5, 3, 4, 7), 4: (0, 1, 2, 3)}
FIRST = (0, -1)
LATE = (0, 1)
ROOT = math.sqrt(2.0 / math.pi)
CUBIC = 0.044715


def places_of(which, steps):
    return tuple(i % steps for i in which)


def dot(left, right, contract=((1,), (0,))):
    return lax.dot_general(left, right, (contract, ((), ())), preferred_element_type=F32)


def kernel(
    order, plane, tile,
    tokens_hbm, gain_hbm, ids_hbm, gates_hbm, cot_hbm, w_in_ref, w_out_ref,
    total, tokens_ref, cot_ref, xhat, scale, columns, g_first, g_second,
    w_first, w_second, sent, landed, gathered, x_rows, d_rows, hidden, d_pre,
    partial, relay, arrived, back, returned, disp, take, rows_in,
    early, spread_in, late_out, home, home_relay, home_in, gain_ref, ids_ref, gates_ref,
    load_sem, disp_send, disp_recv, ag_send, ag_recv, fw_send, fw_recv,
    r1_send, r1_recv, r2_send, r2_recv, ret_send, ret_recv, sp_send, sp_recv, lt_send, lt_recv,
):
    steps = len(order)
    toks, width = tokens_ref.shape
    group = plane * CAP
    both = 2 * group
    chunk = 2 * REPS * group
    chunks = steps // 2
    first = places_of(FIRST, steps)
    lates = places_of(LATE, steps)
    places = steps * plane * UNIT
    me_y = lax.axis_index("rep")
    me_e = lax.axis_index("exp")
    me_z = lax.div(me_e, plane)
    me_p = lax.rem(me_e, plane)
    experts = steps * plane
    up = {"rep": lax.rem(me_y + 1, REPS)}
    down = {"rep": lax.rem(me_y + REPS - 1, REPS)}
    sides = (up, down)

    loads = [
        pltpu.make_async_copy(src, dst, load_sem.at[j])
        for j, (src, dst) in enumerate(
            (
                (tokens_hbm, tokens_ref), (cot_hbm, cot_ref), (w_in_ref, w_first), (w_out_ref, w_second),
                (ids_hbm, ids_ref), (gates_hbm, gates_ref), (gain_hbm, gain_ref),
            )
        )
    ]
    for j in (4, 5, 0, 1, 6):
        loads[j].start()

    barrier = pltpu.get_barrier_semaphore()
    for side in sides:
        pl.semaphore_signal(barrier, inc=1, device_id=side, device_id_type=MESH)

    @pl.loop(1, experts)
    def _(s):
        pl.semaphore_signal(barrier, inc=1, device_id={"exp": lax.rem(me_e + s, experts)}, device_id_type=MESH)

    loads[2].start()
    loads[3].start()

    loads[4].wait()
    loads[5].wait()
    def place_of(k):
        ids = ids_ref[k:k + 1, :]
        z = lax.rem(lax.div(ids, plane) - me_z + steps, steps)
        position = jnp.zeros_like(z)
        for i, away in enumerate(order):
            position = jnp.where(z == away, i, position)
        return position * plane + lax.rem(ids, plane)

    rel = [place_of(k) for k in range(2)]
    labels = lax.broadcasted_iota(jnp.int32, (experts, toks), 0)
    one = [(labels == r).astype(F32) for r in rel]
    earlier = (
        lax.broadcasted_iota(jnp.int32, (toks, toks), 0) < lax.broadcasted_iota(jnp.int32, (toks, toks), 1)
    ).astype(F32).astype(BF16)
    before = dot((one[0] + one[1]).astype(BF16), earlier)
    targets = []
    for k in range(2):
        rank = jnp.sum(before * one[k], axis=0, keepdims=True).astype(jnp.int32)
        targets.append(jnp.where(rank < CAP, rel[k] * UNIT + rank, -UNIT))
    table = jnp.concatenate(
        [t.astype(F32) for t in targets] + [gates_ref[...], jnp.zeros((4, toks), F32)], axis=0
    ).T
    columns[...] = table
    down_q = lax.broadcasted_iota(jnp.int32, (places, toks), 0)
    disp[:, 0:toks] = ((down_q == targets[0]) | (down_q == targets[1])).astype(F32).astype(BF16)
    for k in range(2):
        disp[:, (k + 1) * toks:(k + 2) * toks] = (down_q == targets[k] + CAP).astype(F32).astype(BF16)

    loads[0].wait()
    loads[6].wait()
    values = tokens_ref[...].astype(F32)
    center = values - jnp.mean(values, axis=-1, keepdims=True)
    inv = lax.rsqrt(jnp.mean(center * center, axis=-1, keepdims=True) + EPSILON)
    unit = center * inv
    xhat[...] = unit
    scale[...] = inv
    rows_in[0:toks, :] = (unit * gain_ref[...]).astype(BF16)
    loads[1].wait()
    cot = cot_ref[...].astype(F32)
    for k in range(2):
        rows_in[(k + 1) * toks:(k + 2) * toks, :] = (cot * table[:, 2 + k:3 + k]).astype(BF16)

    def write_take():
        across_q = lax.broadcasted_iota(jnp.int32, (toks, places), 1)
        target = [columns[:, k:k + 1].astype(jnp.int32) for k in range(2)]
        for k in range(2):
            take[k * toks:(k + 1) * toks, :] = (across_q == target[k]).astype(F32).astype(BF16)
        take[2 * toks:3 * toks, :] = (
            (across_q == target[0] + CAP) | (across_q == target[1] + CAP)
        ).astype(F32).astype(BF16)

    def peer(away, p):
        return {"exp": lax.rem(me_z + away + steps, steps) * plane + p}

    rows_at = plane * UNIT

    def dispatch(i):
        piece = dot(disp[i * rows_at:(i + 1) * rows_at, :], rows_in[...])
        piece = piece.reshape(plane, UNIT, width).astype(BF16)
        if i in first:
            early[first.index(i), 0] = piece
        else:
            sent[i] = piece
        if i == 0:
            pl.semaphore_wait(barrier, experts - 1 + 2)
        away = order[i]
        if i in first:
            f = first.index(i)
            for s, slot in ((0, 1), (1, 3)):
                remote(early.at[f, 0], early.at[f, slot], ag_send.at[s], ag_recv.at[s, i], sides[s]).start()
            if i == 0:
                spread(i, 0)
            return
        if away == 0:
            pltpu.make_async_copy(sent.at[i, me_p], landed.at[i, me_p], disp_recv.at[i]).start()

        @pl.loop(1 if away == 0 else 0, plane)
        def _(s):
            p = lax.rem(me_p + s, plane)
            pltpu.make_async_remote_copy(
                sent.at[i, p], landed.at[i, me_p], disp_send.at[i], disp_recv.at[i],
                device_id=peer(away, p), device_id_type=MESH,
            ).start()

    r = lax.broadcasted_iota(jnp.int32, (both, both), 0)
    c = lax.broadcasted_iota(jnp.int32, (both, both), 1)

    def mixed_row(pure):
        kind = lax.div(pure, group)
        row = lax.rem(pure, group)
        return lax.div(row, CAP) * UNIT + kind * CAP + lax.rem(row, CAP)

    def split_perm():
        return (c == mixed_row(r)).astype(F32).astype(BF16)

    def merge_perm():
        return (r == mixed_row(c)).astype(F32).astype(BF16)

    def whole(ref, sem):
        pltpu.make_async_copy(ref, ref, sem).wait()

    def remote(src, dst, send, recv, where):
        return pltpu.make_async_remote_copy(src, dst, send, recv, device_id=where, device_id_type=MESH)

    def arrive(i):
        whole(landed.at[i], disp_recv.at[i])
        units = landed[i].astype(F32).reshape(both, width).astype(BF16)
        gathered[0, i] = dot(split_perm(), units).astype(BF16)
        for s, slot in ((0, 1), (1, 3)):
            remote(gathered.at[0, i], gathered.at[slot, i], ag_send.at[s], ag_recv.at[s, i], sides[s]).start()

    def fan(src, dst, send, recv, away):
        if away == 0:
            pltpu.make_async_copy(src.at[me_p], dst.at[me_p], recv).start()

        @pl.loop(1 if away == 0 else 0, plane)
        def _(s):
            p = lax.rem(me_p + s, plane)
            remote(src.at[p], dst.at[me_p], send, recv, peer(away, p)).start()

    def spread(i, slot):
        f = first.index(i)
        fan(early.at[f, slot], spread_in.at[f, slot], sp_send.at[f, slot], sp_recv.at[f, slot], order[i])

    def forward_early(i):
        f = first.index(i)
        for s, slot in ((0, 1), (1, 3)):
            whole(early.at[f, slot], ag_recv.at[s, i])
            half = pl.ds(s * (plane // 2), plane // 2)
            remote(
                early.at[f, slot, half], early.at[f, 2, half], fw_send.at[s], fw_recv.at[s, i], sides[s]
            ).start()
        if i == 0:
            for slot in (1, 3):
                spread(i, slot)

    def complete_early(i):
        f = first.index(i)
        for s in range(2):
            whole(early.at[f, 2, pl.ds(s * (plane // 2), plane // 2)], fw_recv.at[s, i])
        for slot in ((2,) if i == 0 else (0, 1, 3, 2)):
            spread(i, slot)

    def landed_early(i):
        f = first.index(i)
        for slot in (0, 1, 3, 2):
            whole(spread_in.at[f, slot], sp_recv.at[f, slot])
            units = spread_in[f, slot].astype(F32).reshape(both, width).astype(BF16)
            gathered[slot, i] = dot(split_perm(), units).astype(BF16)

    def forward(i):
        for s, slot in ((0, 1), (1, 3)):
            whole(gathered.at[slot, i], ag_recv.at[s, i])
            half = pl.ds(s * group, group)
            remote(
                gathered.at[slot, i, half], gathered.at[2, i, half], fw_send.at[s], fw_recv.at[s, i], sides[s]
            ).start()

    def complete(i):
        if i in first:
            landed_early(i)
            return
        for s in range(2):
            whole(gathered.at[2, i, pl.ds(s * group, group)], fw_recv.at[s, i])

    def pack(n):
        for rel_y in range(REPS):
            for b in range(2):
                at = n * chunk + (rel_y * 2 + b) * group
                x_rows[at:at + group, :] = gathered[rel_y, 2 * n + b, 0:group, :]
                d_rows[at:at + group, :] = gathered[rel_y, 2 * n + b, group:both, :]

    ff = w_first.shape[1]

    def first_half(n, lo, hi):
        here = pl.ds(n * chunk, chunk)

        @pl.loop(lo, hi)
        def _(t):
            cols = pl.ds(pl.multiple_of(t * tile, tile), tile)
            v = dot(x_rows[here, :], w_first[:, cols])
            g = dot(d_rows[here, :], w_second[cols, :], ((1,), (1,)))
            square = v * v
            th = jnp.tanh(v * (ROOT + (ROOT * CUBIC) * square))
            half_up = 0.5 + 0.5 * th
            hidden[here, cols] = (v * half_up).astype(BF16)
            slope = half_up + (0.5 * v) * (1.0 - th * th) * (ROOT + (3.0 * ROOT * CUBIC) * square)
            d_pre[here, cols] = (g * slope).astype(BF16)

    def second_half(n, lo, hi):
        here = pl.ds(n * chunk, chunk)

        @pl.loop(lo, hi)
        def _(t):
            cols = pl.ds(pl.multiple_of(t * tile, tile), tile)
            y = dot(hidden[here, :], w_second[:, cols]).astype(BF16)
            dx = dot(d_pre[here, :], w_first[cols, :], ((1,), (1,))).astype(BF16)
            for rel_y in range(REPS):
                for b in range(2):
                    at = (rel_y * 2 + b) * group
                    partial[rel_y, 2 * n + b, 0:group, cols] = y[at:at + group]
                    partial[rel_y, 2 * n + b, group:both, cols] = dx[at:at + group]

    opposite = (3, 1)

    def reduce_first(group_ids):
        for i in group_ids:
            for s in range(2):
                half = pl.ds(s * group, group)
                remote(partial.at[2, i, half], relay.at[s, i], r1_send.at[s], r1_recv.at[s, i], sides[s]).start()
        for i in group_ids:
            for s in range(2):
                half = pl.ds((1 - s) * group, group)
                remote(
                    partial.at[opposite[s], i, half], arrived.at[s, i, half], r2_send.at[s], r2_recv.at[s, i], sides[s]
                ).start()

    def reduce_second(i):
        for s in range(2):
            half = pl.ds(s * group, group)
            whole(relay.at[s, i], r1_recv.at[s, i])
            summed = partial[opposite[s], i, half, :].astype(F32) + relay[s, i].astype(F32)
            partial[opposite[s], i, half, :] = summed.astype(BF16)
            remote(
                partial.at[opposite[s], i, half], arrived.at[s, i, half], r2_send.at[s], r2_recv.at[s, i], sides[s]
            ).start()

    def give_back(i):
        for s in range(2):
            whole(arrived.at[s, i], r2_recv.at[s, i])
        summed = partial[0, i].astype(F32) + arrived[0, i].astype(F32) + arrived[1, i].astype(F32)
        back[i] = dot(merge_perm(), summed.astype(BF16)).reshape(plane, UNIT, width).astype(BF16)
        away = order[i]
        if away == 0:
            pltpu.make_async_copy(back.at[i, me_p], returned.at[i, me_p], ret_recv.at[i]).start()

        @pl.loop(1 if away == 0 else 0, plane)
        def _(s):
            p = lax.rem(me_p + s, plane)
            remote(
                back.at[i, p], returned.at[i, me_p], ret_send.at[i], ret_recv.at[i], peer(-away, p)
            ).start()

    def late_send(i):
        l = lates.index(i)
        for slot in (2, 3, 1, 0):
            late_out[l, slot] = dot(merge_perm(), partial[slot, i]).reshape(plane, UNIT, width).astype(BF16)
            fan(late_out.at[l, slot], home.at[l, slot], lt_send.at[l, slot], lt_recv.at[l, slot], -order[i])

    def late_first(i):
        l = lates.index(i)
        whole(home.at[l, 2], lt_recv.at[l, 2])
        for s in range(2):
            half = pl.ds(s * (plane // 2), plane // 2)
            remote(home.at[l, 2, half], home_relay.at[l, s], r1_send.at[s], r1_recv.at[s, i], sides[s]).start()
        for s in range(2):
            whole(home.at[l, opposite[s]], lt_recv.at[l, opposite[s]])
            half = pl.ds((1 - s) * (plane // 2), plane // 2)
            remote(
                home.at[l, opposite[s], half], home_in.at[l, s, half], r2_send.at[s], r2_recv.at[s, i], sides[s]
            ).start()

    def late_second(i):
        l = lates.index(i)
        for s in range(2):
            half = pl.ds(s * (plane // 2), plane // 2)
            whole(home_relay.at[l, s], r1_recv.at[s, i])
            summed = home[l, opposite[s], half].astype(F32) + home_relay[l, s].astype(F32)
            home[l, opposite[s], half] = summed.astype(BF16)
            remote(
                home.at[l, opposite[s], half], home_in.at[l, s, half], r2_send.at[s], r2_recv.at[s, i], sides[s]
            ).start()

    def late_third(i):
        l = lates.index(i)
        whole(home.at[l, 0], lt_recv.at[l, 0])
        for s in range(2):
            whole(home_in.at[l, s], r2_recv.at[s, i])
        summed = home[l, 0].astype(F32) + home_in[l, 0].astype(F32) + home_in[l, 1].astype(F32)
        returned[i] = summed.astype(BF16)

    def combine(n, start):
        for b in range(2):
            if 2 * n + b in lates:
                late_third(2 * n + b)
                continue
            whole(returned.at[2 * n + b], ret_recv.at[2 * n + b])
        span = 2 * rows_at
        units = returned[2 * n:2 * n + 2].astype(F32).reshape(span, width).astype(BF16)
        got = dot(take[:, n * span:(n + 1) * span], units)
        if start:
            total[...] = got
        else:
            total[...] += got

    def out_grad(lo, hi):
        @pl.loop(lo, hi)
        def _(t):
            cols = pl.ds(pl.multiple_of(t * tile, tile), tile)
            g_second[cols, :] = dot(hidden[:, cols], d_rows[...], ((0,), (0,))).astype(BF16)

    def in_grad(lo, hi):
        @pl.loop(lo, hi)
        def _(t):
            cols = pl.ds(pl.multiple_of(t * tile, tile), tile)
            g_first[cols, :] = dot(x_rows[:, cols], d_pre[...], ((0,), (0,))).astype(BF16)

    tiles = ff // tile
    cut = tiles // 2
    normal = [i for i in range(steps) if i not in first]
    ready = iter(normal)
    passed = iter(normal)

    def arrive_next():
        i = next(ready, None)
        if i is not None:
            arrive(i)

    def forward_next():
        i = next(passed, None)
        if i is not None:
            forward(i)

    for i in first:
        dispatch(i)
    for i in normal[:4]:
        dispatch(i)
    write_take()
    forward_early(0)
    for i in normal[4:]:
        dispatch(i)
    arrive_next()
    for i in first[1:]:
        forward_early(i)
    complete_early(0)
    arrive_next()
    forward_next()
    arrive_next()
    for i in first[1:]:
        complete_early(i)
    loads[2].wait()
    loads[3].wait()
    for n in range(chunks):
        pair = (2 * n, 2 * n + 1)
        late = [i for i in pair if i in lates]
        soon = [i for i in pair if i not in lates]
        before = [i for i in (2 * n - 2, 2 * n - 1) if i >= 0 and i not in lates]
        if n == 0:
            forward_next()
        complete(2 * n)
        complete(2 * n + 1)
        pack(n)
        first_half(n, 0, cut)
        arrive_next()
        for i in before[:1]:
            reduce_second(i)
        first_half(n, cut, tiles)
        forward_next()
        for i in before[1:]:
            reduce_second(i)
        second_half(n, 0, cut)
        arrive_next()
        second_half(n, cut, tiles)
        reduce_first(soon)
        forward_next()
        for i in late:
            late_send(i)
        for i in before:
            give_back(i)
        if n == chunks - 1:
            out_grad(0, cut)
    out_grad(cut, tiles)
    for i in (steps - 2, steps - 1):
        reduce_second(i)
    for i in lates:
        late_first(i)
    in_grad(0, cut)
    for i in (steps - 2, steps - 1):
        give_back(i)
    for i in lates:
        late_second(i)
    in_grad(cut, tiles)
    finals = list(range(1, chunks - 1)) + [0, chunks - 1]
    for n in finals:
        combine(n, n == finals[0])

    for i in range(steps):
        for buf, sem, other in ((sent, disp_send, first), (back, ret_send, lates)):
            if i in other:
                continue
            whole(buf.at[i, 0:plane - 1] if order[i] == 0 else buf.at[i], sem.at[i])
    for buf, sem, which in ((early, sp_send, first), (late_out, lt_send, lates)):
        for j, i in enumerate(which):
            for slot in range(REPS):
                whole(buf.at[j, slot, 0:plane - 1] if order[i] == 0 else buf.at[j, slot], sem.at[j, slot])
    for s in range(2):
        whole(gathered.at[0], ag_send.at[s])
        whole(gathered.at[0, :, pl.ds(0, group)], fw_send.at[s])
        whole(partial.at[0, :, pl.ds(0, group)], r1_send.at[s])
        whole(partial.at[0], r2_send.at[s])


def finish(
    total, tokens_ref, cot_ref, xhat, scale, columns, g_first, g_second, gain_ref,
    mixed_ref, grad_tokens_ref, grad_in_ref, grad_out_ref, mixed, grad_tokens, store_sem,
):
    toks = tokens_ref.shape[0]
    stores = [
        pltpu.make_async_copy(src, dst, store_sem.at[j])
        for j, (src, dst) in enumerate((
            (g_first, grad_in_ref), (g_second, grad_out_ref), (mixed, mixed_ref), (grad_tokens, grad_tokens_ref),
        ))
    ]
    stores[0].start()
    stores[1].start()
    picked = total[0:toks, :] * columns[:, 2:3] + total[toks:2 * toks, :] * columns[:, 3:4]
    mixed[...] = (tokens_ref[...].astype(F32) + picked).astype(BF16)
    stores[2].start()
    g = total[2 * toks:3 * toks, :] * gain_ref[...]
    unit = xhat[...]
    inner = g - jnp.mean(g, axis=-1, keepdims=True) - unit * jnp.mean(g * unit, axis=-1, keepdims=True)
    grad_tokens[...] = (cot_ref[...].astype(F32) + scale[...] * inner).astype(BF16)
    stores[3].start()
    for store in stores:
        store.wait()


def local(plane, tokens, gain, expert_ids, gates, w_in, w_out, cotangent):
    experts = lax.axis_size("exp")
    steps = experts // plane
    order = ORDERS[steps]
    toks, width = tokens.shape
    ff = w_in.shape[2]
    group = plane * CAP
    rows = experts * CAP * REPS
    places = experts * UNIT
    dma = pltpu.SemaphoreType.DMA
    vmem = pl.BlockSpec(memory_space=pltpu.VMEM)
    hbm = pl.BlockSpec(memory_space=pl.ANY)
    unit = (steps, plane, UNIT, width)
    held = pl.pallas_call(
        functools.partial(kernel, order, plane, min(256, ff // 2)),
        out_shape=(
            pltpu.VMEM((3 * toks, width), F32),
            pltpu.VMEM((toks, width), BF16),
            pltpu.VMEM((toks, width), BF16),
            pltpu.VMEM((toks, width), F32),
            pltpu.VMEM((toks, 1), F32),
            pltpu.VMEM((toks, 8), F32),
            pltpu.VMEM((width, ff), BF16),
            pltpu.VMEM((ff, width), BF16),
        ),
        in_specs=[hbm] * 7,
        out_specs=(vmem,) * 8,
        scratch_shapes=[
            pltpu.VMEM((width, ff), BF16),
            pltpu.VMEM((ff, width), BF16),
            pltpu.VMEM(unit, BF16),
            pltpu.VMEM(unit, BF16),
            pltpu.VMEM((REPS, steps, 2 * group, width), BF16),
            pltpu.VMEM((rows, width), BF16),
            pltpu.VMEM((rows, width), BF16),
            pltpu.VMEM((rows, ff), BF16),
            pltpu.VMEM((rows, ff), BF16),
            pltpu.VMEM((REPS, steps, 2 * group, width), BF16),
            pltpu.VMEM((2, steps, group, width), BF16),
            pltpu.VMEM((2, steps, 2 * group, width), BF16),
            pltpu.VMEM(unit, BF16),
            pltpu.VMEM(unit, BF16),
            pltpu.VMEM((places, 3 * toks), BF16),
            pltpu.VMEM((3 * toks, places), BF16),
            pltpu.VMEM((3 * toks, width), BF16),
            pltpu.VMEM((len(FIRST), REPS) + unit[1:], BF16),
            pltpu.VMEM((len(FIRST), REPS) + unit[1:], BF16),
            pltpu.VMEM((len(LATE), REPS) + unit[1:], BF16),
            pltpu.VMEM((len(LATE), REPS) + unit[1:], BF16),
            pltpu.VMEM((len(LATE), 2, plane // 2, UNIT, width), BF16),
            pltpu.VMEM((len(LATE), 2) + unit[1:], BF16),
            pltpu.VMEM((1, width), F32),
            pltpu.VMEM((2, toks), jnp.int32),
            pltpu.VMEM((2, toks), F32),
            dma((7,)),
            dma((steps,)),
            dma((steps,)),
            dma((2,)),
            dma((2, steps)),
            dma((2,)),
            dma((2, steps)),
            dma((2,)),
            dma((2, steps)),
            dma((2,)),
            dma((2, steps)),
            dma((steps,)),
            dma((steps,)),
            dma((len(FIRST), REPS)),
            dma((len(FIRST), REPS)),
            dma((len(LATE), REPS)),
            dma((len(LATE), REPS)),
        ],
        compiler_params=pltpu.CompilerParams(
            collective_id=0, has_side_effects=True, vmem_limit_bytes=53 * 1024 * 1024
        ),
    )(tokens, gain.reshape(1, width), expert_ids.T, gates.T, cotangent, w_in[0], w_out[0])
    mixed, grad_tokens, grad_in, grad_out = pl.pallas_call(
        finish,
        out_shape=(
            jax.ShapeDtypeStruct((toks, width), BF16),
            jax.ShapeDtypeStruct((toks, width), BF16),
            jax.ShapeDtypeStruct((width, ff), BF16),
            jax.ShapeDtypeStruct((ff, width), BF16),
        ),
        in_specs=[vmem] * 9,
        out_specs=(hbm,) * 4,
        scratch_shapes=[
            pltpu.VMEM((toks, width), BF16),
            pltpu.VMEM((toks, width), BF16),
            dma((4,)),
        ],
        compiler_params=pltpu.CompilerParams(vmem_limit_bytes=16 * 1024 * 1024),
    )(*[pltpu.with_memory_space_constraint(h, pltpu.VMEM) for h in held], gain.reshape(1, width))
    return (mixed, grad_tokens, grad_in[None], grad_out[None])


def solution(mesh, plane=PLANE):
    return jax.shard_map(
        functools.partial(local, plane),
        mesh=mesh,
        in_specs=(
            P(("rep", "exp"), None),
            P(),
            P(("rep", "exp"), None),
            P(("rep", "exp"), None),
            P("exp", None, "rep"),
            P("exp", "rep", None),
            P(("rep", "exp"), None),
        ),
        out_specs=(
            P(("rep", "exp"), None),
            P(("rep", "exp"), None),
            P("exp", None, "rep"),
            P("exp", "rep", None),
        ),
        check_vma=False,
    )
```

```python
import functools
import math

import jax
import jax.numpy as jnp
from jax import lax
from jax.experimental import pallas as pl
from jax.experimental.pallas import tpu as pltpu
from jax.sharding import PartitionSpec as P

MESH = pl.DeviceIdType.MESH
F32 = jnp.float32
BF16 = jnp.bfloat16
EPSILON = 1e-05
CAP = 4
UNIT = 2 * CAP
REPS = 4
PLANE = 8
ORDERS = {8: (0, 1, 6, 2, 5, 3, 4, 7), 4: (0, 1, 2, 3)}
FIRST = (0, -1)
LATE = (0, 1)
ROOT = math.sqrt(2.0 / math.pi)
CUBIC = 0.044715


def places_of(which, steps):
    return tuple(i % steps for i in which)


def dot(left, right, contract=((1,), (0,))):
    return lax.dot_general(left, right, (contract, ((), ())), preferred_element_type=F32)


def kernel(
    order, plane, tile,
    tokens_hbm, gain_hbm, ids_hbm, gates_hbm, cot_hbm, w_in_ref, w_out_ref,
    total, tokens_ref, cot_ref, xhat, scale, columns, g_first, g_second,
    w_first, w_second, sent, landed, gathered, x_rows, d_rows, hidden, d_pre,
    partial, relay, arrived, back, returned, disp, take, rows_in,
    early, spread_in, late_out, home, home_relay, home_in, gain_ref, ids_ref, gates_ref,
    load_sem, disp_send, disp_recv, ag_send, ag_recv, fw_send, fw_recv,
    r1_send, r1_recv, r2_send, r2_recv, ret_send, ret_recv, sp_send, sp_recv, lt_send, lt_recv,
):
    steps = len(order)
    toks, width = tokens_ref.shape
    group = plane * CAP
    both = 2 * group
    chunk = 2 * REPS * group
    chunks = steps // 2
    first = places_of(FIRST, steps)
    lates = places_of(LATE, steps)
    places = steps * plane * UNIT
    me_y = lax.axis_index("rep")
    me_e = lax.axis_index("exp")
    me_z = lax.div(me_e, plane)
    me_p = lax.rem(me_e, plane)
    experts = steps * plane
    up = {"rep": lax.rem(me_y + 1, REPS)}
    down = {"rep": lax.rem(me_y + REPS - 1, REPS)}
    sides = (up, down)

    loads = [
        pltpu.make_async_copy(src, dst, load_sem.at[j])
        for j, (src, dst) in enumerate(
            (
                (tokens_hbm, tokens_ref), (cot_hbm, cot_ref), (w_in_ref, w_first), (w_out_ref, w_second),
                (ids_hbm, ids_ref), (gates_hbm, gates_ref), (gain_hbm, gain_ref),
            )
        )
    ]
    for j in (4, 5, 0, 1, 6):
        loads[j].start()

    barrier = pltpu.get_barrier_semaphore()
    for side in sides:
        pl.semaphore_signal(barrier, inc=1, device_id=side, device_id_type=MESH)

    @pl.loop(1, experts)
    def _(s):
        pl.semaphore_signal(barrier, inc=1, device_id={"exp": lax.rem(me_e + s, experts)}, device_id_type=MESH)

    loads[2].start()
    loads[3].start()

    loads[4].wait()
    loads[5].wait()
    def place_of(k):
        ids = ids_ref[k:k + 1, :]
        z = lax.rem(lax.div(ids, plane) - me_z + steps, steps)
        position = jnp.zeros_like(z)
        for i, away in enumerate(order):
            position = jnp.where(z == away, i, position)
        return position * plane + lax.rem(ids, plane)

    rel = [place_of(k) for k in range(2)]
    labels = lax.broadcasted_iota(jnp.int32, (experts, toks), 0)
    one = [(labels == r).astype(F32) for r in rel]
    earlier = (
        lax.broadcasted_iota(jnp.int32, (toks, toks), 0) < lax.broadcasted_iota(jnp.int32, (toks, toks), 1)
    ).astype(F32).astype(BF16)
    before = dot((one[0] + one[1]).astype(BF16), earlier)
    targets = []
    for k in range(2):
        rank = jnp.sum(before * one[k], axis=0, keepdims=True).astype(jnp.int32)
        targets.append(jnp.where(rank < CAP, rel[k] * UNIT + rank, -UNIT))
    table = jnp.concatenate(
        [t.astype(F32) for t in targets] + [gates_ref[...], jnp.zeros((4, toks), F32)], axis=0
    ).T
    columns[...] = table
    down_q = lax.broadcasted_iota(jnp.int32, (places, toks), 0)
    disp[:, 0:toks] = ((down_q == targets[0]) | (down_q == targets[1])).astype(F32).astype(BF16)
    for k in range(2):
        disp[:, (k + 1) * toks:(k + 2) * toks] = (down_q == targets[k] + CAP).astype(F32).astype(BF16)

    loads[0].wait()
    loads[6].wait()
    values = tokens_ref[...].astype(F32)
    center = values - jnp.mean(values, axis=-1, keepdims=True)
    inv = lax.rsqrt(jnp.mean(center * center, axis=-1, keepdims=True) + EPSILON)
    unit = center * inv
    xhat[...] = unit
    scale[...] = inv
    rows_in[0:toks, :] = (unit * gain_ref[...]).astype(BF16)
    loads[1].wait()
    cot = cot_ref[...].astype(F32)
    for k in range(2):
        rows_in[(k + 1) * toks:(k + 2) * toks, :] = (cot * table[:, 2 + k:3 + k]).astype(BF16)

    def write_take():
        across_q = lax.broadcasted_iota(jnp.int32, (toks, places), 1)
        target = [columns[:, k:k + 1].astype(jnp.int32) for k in range(2)]
        for k in range(2):
            take[k * toks:(k + 1) * toks, :] = (across_q == target[k]).astype(F32).astype(BF16)
        take[2 * toks:3 * toks, :] = (
            (across_q == target[0] + CAP) | (across_q == target[1] + CAP)
        ).astype(F32).astype(BF16)

    def peer(away, p):
        return {"exp": lax.rem(me_z + away + steps, steps) * plane + p}

    rows_at = plane * UNIT

    def dispatch(i):
        piece = dot(disp[i * rows_at:(i + 1) * rows_at, :], rows_in[...])
        piece = piece.reshape(plane, UNIT, width).astype(BF16)
        if i in first:
            early[first.index(i), 0] = piece
        else:
            sent[i] = piece
        if i == 0:
            pl.semaphore_wait(barrier, experts - 1 + 2)
        away = order[i]
        if i in first:
            f = first.index(i)
            for s, slot in ((0, 1), (1, 3)):
                remote(early.at[f, 0], early.at[f, slot], ag_send.at[s], ag_recv.at[s, i], sides[s]).start()
            if i == 0:
                spread(i, 0)
            return
        if away == 0:
            pltpu.make_async_copy(sent.at[i, me_p], landed.at[i, me_p], disp_recv.at[i]).start()

        @pl.loop(1 if away == 0 else 0, plane)
        def _(s):
            p = lax.rem(me_p + s, plane)
            pltpu.make_async_remote_copy(
                sent.at[i, p], landed.at[i, me_p], disp_send.at[i], disp_recv.at[i],
                device_id=peer(away, p), device_id_type=MESH,
            ).start()

    r = lax.broadcasted_iota(jnp.int32, (both, both), 0)
    c = lax.broadcasted_iota(jnp.int32, (both, both), 1)

    def mixed_row(pure):
        kind = lax.div(pure, group)
        row = lax.rem(pure, group)
        return lax.div(row, CAP) * UNIT + kind * CAP + lax.rem(row, CAP)

    def split_perm():
        return (c == mixed_row(r)).astype(F32).astype(BF16)

    def merge_perm():
        return (r == mixed_row(c)).astype(F32).astype(BF16)

    def whole(ref, sem):
        pltpu.make_async_copy(ref, ref, sem).wait()

    def remote(src, dst, send, recv, where):
        return pltpu.make_async_remote_copy(src, dst, send, recv, device_id=where, device_id_type=MESH)

    def arrive(i):
        whole(landed.at[i], disp_recv.at[i])
        units = landed[i].astype(F32).reshape(both, width).astype(BF16)
        gathered[0, i] = dot(split_perm(), units).astype(BF16)
        for s, slot in ((0, 1), (1, 3)):
            remote(gathered.at[0, i], gathered.at[slot, i], ag_send.at[s], ag_recv.at[s, i], sides[s]).start()

    def fan(src, dst, send, recv, away):
        if away == 0:
            pltpu.make_async_copy(src.at[me_p], dst.at[me_p], recv).start()

        @pl.loop(1 if away == 0 else 0, plane)
        def _(s):
            p = lax.rem(me_p + s, plane)
            remote(src.at[p], dst.at[me_p], send, recv, peer(away, p)).start()

    def spread(i, slot):
        f = first.index(i)
        fan(early.at[f, slot], spread_in.at[f, slot], sp_send.at[f, slot], sp_recv.at[f, slot], order[i])

    def forward_early(i):
        f = first.index(i)
        for s, slot in ((0, 1), (1, 3)):
            whole(early.at[f, slot], ag_recv.at[s, i])
            half = pl.ds(s * (plane // 2), plane // 2)
            remote(
                early.at[f, slot, half], early.at[f, 2, half], fw_send.at[s], fw_recv.at[s, i], sides[s]
            ).start()
        if i == 0:
            for slot in (1, 3):
                spread(i, slot)

    def complete_early(i):
        f = first.index(i)
        for s in range(2):
            whole(early.at[f, 2, pl.ds(s * (plane // 2), plane // 2)], fw_recv.at[s, i])
        for slot in ((2,) if i == 0 else (0, 1, 3, 2)):
            spread(i, slot)

    def landed_early(i):
        f = first.index(i)
        for slot in (0, 1, 3, 2):
            whole(spread_in.at[f, slot], sp_recv.at[f, slot])
            units = spread_in[f, slot].astype(F32).reshape(both, width).astype(BF16)
            gathered[slot, i] = dot(split_perm(), units).astype(BF16)

    def forward(i):
        for s, slot in ((0, 1), (1, 3)):
            whole(gathered.at[slot, i], ag_recv.at[s, i])
            half = pl.ds(s * group, group)
            remote(
                gathered.at[slot, i, half], gathered.at[2, i, half], fw_send.at[s], fw_recv.at[s, i], sides[s]
            ).start()

    def complete(i):
        if i in first:
            landed_early(i)
            return
        for s in range(2):
            whole(gathered.at[2, i, pl.ds(s * group, group)], fw_recv.at[s, i])

    def pack(n):
        for rel_y in range(REPS):
            for b in range(2):
                at = n * chunk + (rel_y * 2 + b) * group
                x_rows[at:at + group, :] = gathered[rel_y, 2 * n + b, 0:group, :]
                d_rows[at:at + group, :] = gathered[rel_y, 2 * n + b, group:both, :]

    ff = w_first.shape[1]

    def first_half(n, lo, hi):
        here = pl.ds(n * chunk, chunk)

        @pl.loop(lo, hi)
        def _(t):
            cols = pl.ds(pl.multiple_of(t * tile, tile), tile)
            v = dot(x_rows[here, :], w_first[:, cols])
            g = dot(d_rows[here, :], w_second[cols, :], ((1,), (1,)))
            square = v * v
            th = jnp.tanh(v * (ROOT + (ROOT * CUBIC) * square))
            half_up = 0.5 + 0.5 * th
            hidden[here, cols] = (v * half_up).astype(BF16)
            slope = half_up + (0.5 * v) * (1.0 - th * th) * (ROOT + (3.0 * ROOT * CUBIC) * square)
            d_pre[here, cols] = (g * slope).astype(BF16)

    def second_half(n, lo, hi):
        here = pl.ds(n * chunk, chunk)

        @pl.loop(lo, hi)
        def _(t):
            cols = pl.ds(pl.multiple_of(t * tile, tile), tile)
            y = dot(hidden[here, :], w_second[:, cols]).astype(BF16)
            dx = dot(d_pre[here, :], w_first[cols, :], ((1,), (1,))).astype(BF16)
            for rel_y in range(REPS):
                for b in range(2):
                    at = (rel_y * 2 + b) * group
                    partial[rel_y, 2 * n + b, 0:group, cols] = y[at:at + group]
                    partial[rel_y, 2 * n + b, group:both, cols] = dx[at:at + group]

    opposite = (3, 1)

    def reduce_first(group_ids):
        for i in group_ids:
            for s in range(2):
                half = pl.ds(s * group, group)
                remote(partial.at[2, i, half], relay.at[s, i], r1_send.at[s], r1_recv.at[s, i], sides[s]).start()
        for i in group_ids:
            for s in range(2):
                half = pl.ds((1 - s) * group, group)
                remote(
                    partial.at[opposite[s], i, half], arrived.at[s, i, half], r2_send.at[s], r2_recv.at[s, i], sides[s]
                ).start()

    def reduce_second(i):
        for s in range(2):
            half = pl.ds(s * group, group)
            whole(relay.at[s, i], r1_recv.at[s, i])
            summed = partial[opposite[s], i, half, :].astype(F32) + relay[s, i].astype(F32)
            partial[opposite[s], i, half, :] = summed.astype(BF16)
            remote(
                partial.at[opposite[s], i, half], arrived.at[s, i, half], r2_send.at[s], r2_recv.at[s, i], sides[s]
            ).start()

    def give_back(i):
        for s in range(2):
            whole(arrived.at[s, i], r2_recv.at[s, i])
        summed = partial[0, i].astype(F32) + arrived[0, i].astype(F32) + arrived[1, i].astype(F32)
        back[i] = dot(merge_perm(), summed.astype(BF16)).reshape(plane, UNIT, width).astype(BF16)
        away = order[i]
        if away == 0:
            pltpu.make_async_copy(back.at[i, me_p], returned.at[i, me_p], ret_recv.at[i]).start()

        @pl.loop(1 if away == 0 else 0, plane)
        def _(s):
            p = lax.rem(me_p + s, plane)
            remote(
                back.at[i, p], returned.at[i, me_p], ret_send.at[i], ret_recv.at[i], peer(-away, p)
            ).start()

    def late_send(i):
        l = lates.index(i)
        for slot in (2, 3, 1, 0):
            late_out[l, slot] = dot(merge_perm(), partial[slot, i]).reshape(plane, UNIT, width).astype(BF16)
            fan(late_out.at[l, slot], home.at[l, slot], lt_send.at[l, slot], lt_recv.at[l, slot], -order[i])

    def late_first(i):
        l = lates.index(i)
        whole(home.at[l, 2], lt_recv.at[l, 2])
        for s in range(2):
            half = pl.ds(s * (plane // 2), plane // 2)
            remote(home.at[l, 2, half], home_relay.at[l, s], r1_send.at[s], r1_recv.at[s, i], sides[s]).start()
        for s in range(2):
            whole(home.at[l, opposite[s]], lt_recv.at[l, opposite[s]])
            half = pl.ds((1 - s) * (plane // 2), plane // 2)
            remote(
                home.at[l, opposite[s], half], home_in.at[l, s, half], r2_send.at[s], r2_recv.at[s, i], sides[s]
            ).start()

    def late_second(i):
        l = lates.index(i)
        for s in range(2):
            half = pl.ds(s * (plane // 2), plane // 2)
            whole(home_relay.at[l, s], r1_recv.at[s, i])
            summed = home[l, opposite[s], half].astype(F32) + home_relay[l, s].astype(F32)
            home[l, opposite[s], half] = summed.astype(BF16)
            remote(
                home.at[l, opposite[s], half], home_in.at[l, s, half], r2_send.at[s], r2_recv.at[s, i], sides[s]
            ).start()

    def late_third(i):
        l = lates.index(i)
        whole(home.at[l, 0], lt_recv.at[l, 0])
        for s in range(2):
            whole(home_in.at[l, s], r2_recv.at[s, i])
        summed = home[l, 0].astype(F32) + home_in[l, 0].astype(F32) + home_in[l, 1].astype(F32)
        returned[i] = summed.astype(BF16)

    def combine(n, start):
        for b in range(2):
            if 2 * n + b in lates:
                late_third(2 * n + b)
                continue
            whole(returned.at[2 * n + b], ret_recv.at[2 * n + b])
        span = 2 * rows_at
        units = returned[2 * n:2 * n + 2].astype(F32).reshape(span, width).astype(BF16)
        got = dot(take[:, n * span:(n + 1) * span], units)
        if start:
            total[...] = got
        else:
            total[...] += got

    def out_grad(lo, hi):
        @pl.loop(lo, hi)
        def _(t):
            cols = pl.ds(pl.multiple_of(t * tile, tile), tile)
            g_second[cols, :] = dot(hidden[:, cols], d_rows[...], ((0,), (0,))).astype(BF16)

    def in_grad(lo, hi):
        @pl.loop(lo, hi)
        def _(t):
            cols = pl.ds(pl.multiple_of(t * tile, tile), tile)
            g_first[cols, :] = dot(x_rows[:, cols], d_pre[...], ((0,), (0,))).astype(BF16)

    tiles = ff // tile
    cut = tiles // 2
    normal = [i for i in range(steps) if i not in first]
    ready = iter(normal)
    passed = iter(normal)

    def arrive_next():
        i = next(ready, None)
        if i is not None:
            arrive(i)

    def forward_next():
        i = next(passed, None)
        if i is not None:
            forward(i)

    dispatch(0)
    dispatch(normal[0])
    for i in first[1:]:
        dispatch(i)
    for i in normal[1:4]:
        dispatch(i)
    write_take()
    forward_early(0)
    for i in normal[4:]:
        dispatch(i)
    arrive_next()
    for i in first[1:]:
        forward_early(i)
    complete_early(0)
    arrive_next()
    forward_next()
    arrive_next()
    for i in first[1:]:
        complete_early(i)
    loads[2].wait()
    loads[3].wait()
    for n in range(chunks):
        pair = (2 * n, 2 * n + 1)
        late = [i for i in pair if i in lates]
        soon = [i for i in pair if i not in lates]
        before = [i for i in (2 * n - 2, 2 * n - 1) if i >= 0 and i not in lates]
        if n == 0:
            forward_next()
        complete(2 * n)
        complete(2 * n + 1)
        pack(n)
        first_half(n, 0, cut)
        arrive_next()
        for i in before[:1]:
            reduce_second(i)
        first_half(n, cut, tiles)
        forward_next()
        for i in before[1:]:
            reduce_second(i)
        second_half(n, 0, cut)
        arrive_next()
        second_half(n, cut, tiles)
        reduce_first(soon)
        forward_next()
        for i in late:
            late_send(i)
        for i in before:
            give_back(i)
        if n == chunks - 1:
            out_grad(0, cut)
    out_grad(cut, tiles)
    for i in (steps - 2, steps - 1):
        reduce_second(i)
    for i in lates:
        late_first(i)
    in_grad(0, cut)
    for i in (steps - 2, steps - 1):
        give_back(i)
    for i in lates:
        late_second(i)
    in_grad(cut, tiles)
    finals = list(range(1, chunks - 1)) + [0, chunks - 1]
    for n in finals:
        combine(n, n == finals[0])

    for i in range(steps):
        for buf, sem, other in ((sent, disp_send, first), (back, ret_send, lates)):
            if i in other:
                continue
            whole(buf.at[i, 0:plane - 1] if order[i] == 0 else buf.at[i], sem.at[i])
    for buf, sem, which in ((early, sp_send, first), (late_out, lt_send, lates)):
        for j, i in enumerate(which):
            for slot in range(REPS):
                whole(buf.at[j, slot, 0:plane - 1] if order[i] == 0 else buf.at[j, slot], sem.at[j, slot])
    for s in range(2):
        whole(gathered.at[0], ag_send.at[s])
        whole(gathered.at[0, :, pl.ds(0, group)], fw_send.at[s])
        whole(partial.at[0, :, pl.ds(0, group)], r1_send.at[s])
        whole(partial.at[0], r2_send.at[s])


def finish(
    total, tokens_ref, cot_ref, xhat, scale, columns, g_first, g_second, gain_ref,
    mixed_ref, grad_tokens_ref, grad_in_ref, grad_out_ref, mixed, grad_tokens, store_sem,
):
    toks = tokens_ref.shape[0]
    stores = [
        pltpu.make_async_copy(src, dst, store_sem.at[j])
        for j, (src, dst) in enumerate((
            (g_first, grad_in_ref), (g_second, grad_out_ref), (mixed, mixed_ref), (grad_tokens, grad_tokens_ref),
        ))
    ]
    stores[0].start()
    stores[1].start()
    picked = total[0:toks, :] * columns[:, 2:3] + total[toks:2 * toks, :] * columns[:, 3:4]
    mixed[...] = (tokens_ref[...].astype(F32) + picked).astype(BF16)
    stores[2].start()
    g = total[2 * toks:3 * toks, :] * gain_ref[...]
    unit = xhat[...]
    inner = g - jnp.mean(g, axis=-1, keepdims=True) - unit * jnp.mean(g * unit, axis=-1, keepdims=True)
    grad_tokens[...] = (cot_ref[...].astype(F32) + scale[...] * inner).astype(BF16)
    stores[3].start()
    for store in stores:
        store.wait()


def local(plane, tokens, gain, expert_ids, gates, w_in, w_out, cotangent):
    experts = lax.axis_size("exp")
    steps = experts // plane
    order = ORDERS[steps]
    toks, width = tokens.shape
    ff = w_in.shape[2]
    group = plane * CAP
    rows = experts * CAP * REPS
    places = experts * UNIT
    dma = pltpu.SemaphoreType.DMA
    vmem = pl.BlockSpec(memory_space=pltpu.VMEM)
    hbm = pl.BlockSpec(memory_space=pl.ANY)
    unit = (steps, plane, UNIT, width)
    held = pl.pallas_call(
        functools.partial(kernel, order, plane, min(256, ff // 2)),
        out_shape=(
            pltpu.VMEM((3 * toks, width), F32),
            pltpu.VMEM((toks, width), BF16),
            pltpu.VMEM((toks, width), BF16),
            pltpu.VMEM((toks, width), F32),
            pltpu.VMEM((toks, 1), F32),
            pltpu.VMEM((toks, 8), F32),
            pltpu.VMEM((width, ff), BF16),
            pltpu.VMEM((ff, width), BF16),
        ),
        in_specs=[hbm] * 7,
        out_specs=(vmem,) * 8,
        scratch_shapes=[
            pltpu.VMEM((width, ff), BF16),
            pltpu.VMEM((ff, width), BF16),
            pltpu.VMEM(unit, BF16),
            pltpu.VMEM(unit, BF16),
            pltpu.VMEM((REPS, steps, 2 * group, width), BF16),
            pltpu.VMEM((rows, width), BF16),
            pltpu.VMEM((rows, width), BF16),
            pltpu.VMEM((rows, ff), BF16),
            pltpu.VMEM((rows, ff), BF16),
            pltpu.VMEM((REPS, steps, 2 * group, width), BF16),
            pltpu.VMEM((2, steps, group, width), BF16),
            pltpu.VMEM((2, steps, 2 * group, width), BF16),
            pltpu.VMEM(unit, BF16),
            pltpu.VMEM(unit, BF16),
            pltpu.VMEM((places, 3 * toks), BF16),
            pltpu.VMEM((3 * toks, places), BF16),
            pltpu.VMEM((3 * toks, width), BF16),
            pltpu.VMEM((len(FIRST), REPS) + unit[1:], BF16),
            pltpu.VMEM((len(FIRST), REPS) + unit[1:], BF16),
            pltpu.VMEM((len(LATE), REPS) + unit[1:], BF16),
            pltpu.VMEM((len(LATE), REPS) + unit[1:], BF16),
            pltpu.VMEM((len(LATE), 2, plane // 2, UNIT, width), BF16),
            pltpu.VMEM((len(LATE), 2) + unit[1:], BF16),
            pltpu.VMEM((1, width), F32),
            pltpu.VMEM((2, toks), jnp.int32),
            pltpu.VMEM((2, toks), F32),
            dma((7,)),
            dma((steps,)),
            dma((steps,)),
            dma((2,)),
            dma((2, steps)),
            dma((2,)),
            dma((2, steps)),
            dma((2,)),
            dma((2, steps)),
            dma((2,)),
            dma((2, steps)),
            dma((steps,)),
            dma((steps,)),
            dma((len(FIRST), REPS)),
            dma((len(FIRST), REPS)),
            dma((len(LATE), REPS)),
            dma((len(LATE), REPS)),
        ],
        compiler_params=pltpu.CompilerParams(
            collective_id=0, has_side_effects=True, vmem_limit_bytes=53 * 1024 * 1024
        ),
    )(tokens, gain.reshape(1, width), expert_ids.T, gates.T, cotangent, w_in[0], w_out[0])
    mixed, grad_tokens, grad_in, grad_out = pl.pallas_call(
        finish,
        out_shape=(
            jax.ShapeDtypeStruct((toks, width), BF16),
            jax.ShapeDtypeStruct((toks, width), BF16),
            jax.ShapeDtypeStruct((width, ff), BF16),
            jax.ShapeDtypeStruct((ff, width), BF16),
        ),
        in_specs=[vmem] * 9,
        out_specs=(hbm,) * 4,
        scratch_shapes=[
            pltpu.VMEM((toks, width), BF16),
            pltpu.VMEM((toks, width), BF16),
            dma((4,)),
        ],
        compiler_params=pltpu.CompilerParams(vmem_limit_bytes=16 * 1024 * 1024),
    )(*[pltpu.with_memory_space_constraint(h, pltpu.VMEM) for h in held], gain.reshape(1, width))
    return (mixed, grad_tokens, grad_in[None], grad_out[None])


def solution(mesh, plane=PLANE):
    return jax.shard_map(
        functools.partial(local, plane),
        mesh=mesh,
        in_specs=(
            P(("rep", "exp"), None),
            P(),
            P(("rep", "exp"), None),
            P(("rep", "exp"), None),
            P("exp", None, "rep"),
            P("exp", "rep", None),
            P(("rep", "exp"), None),
        ),
        out_specs=(
            P(("rep", "exp"), None),
            P(("rep", "exp"), None),
            P("exp", None, "rep"),
            P("exp", "rep", None),
        ),
        check_vma=False,
    )
```
